256 devices in a mesh: dp: 128 (over z, y, x), mp: 2 (over core).
Axes of the slice: x: 4, y: 4, z: 8, core: 2. Of those that a mesh axis runs over, the one named last changes fastest.
Arguments:
- acts: bfloat16 [131072, 4096], P('dp', 'mp'), may hold values from -6 to 6
- cotangent: bfloat16 [131072, 1024], P('dp', 'mp'), may hold values from -6 to 6
- value_weight: bfloat16 [1024, 4096], P(None, 'mp'), may hold values from -0.1875 to 0.1875
- proj_in: bfloat16 [64, 4096], P(None, 'mp'), may hold values from -0.09375 to 0.09375
- proj_out: bfloat16 [64, 1024], replicated, may hold values from -0.1875 to 0.1875
- query_grads: bfloat16 [512, 4096], P('dp', 'mp'), may hold values from -0.01171875 to 0.01171875
- lengths: int32 [1024], P('dp'), may hold values from 1 to 256, as said below
- plan: int32 [16384, 2], P('dp'), may hold values from 0 to 640, as said below
- corpus: int32 [1024], P('dp'), may hold values from 0 to 1023, as said below
- segments: int32 [131072], P('dp'), may hold values from 0 to 8, as said below
Outputs:
- input_grad: bfloat16 [131072, 4096], P('dp', 'mp')
- balanced: bfloat16 [81920, 128], P('dp')
- influence: float32 [1024, 512], P('dp', 'mp')
The draws below stay inside these ranges and needn't reach their ends.
Inputs may be any that keep to these rules, and one draw needn't show every extreme that they name: `lengths`: the documents of a device lie in number order from its first token slot; the slots after them are padding. The live tokens of each device number a multiple of 8, and every device holds one document of exactly 256 tokens. For a block of live token slots, plan[k, 0] is its balanced device and plan[k, 1] its first row there, a multiple of 8; the blocks sent to one balanced device fill its 640 rows exactly, without gaps or intersection. At most 1 block of one device go to one balanced device, and that many do. Padding blocks hold (0, 640). `corpus`: A permutation of the documents; index c is owned by device c // 8 of dp. The documents of one device all have different owners. `segments`: each slot holds the device-local number of the document that the lengths place there, or 8 on padding.
All inputs are finite; a program needn't handle non-finite values.
Results may differ from the reference program's by a relative error of at most 0.015.
Values may be sent and summed in bfloat16 or wider, within the bound.
No kernel may reach another device: no remote copies, remote signals or barrier semaphores. Data moves between devices by JAX's collectives and lax.ppermute only.
A program may use at most 64 MiB of HBM per device.

```python
import jax
import jax.numpy as jnp
from jax import lax

D = 4096
KV = 1024
R = 64
Q = 512
LMAX = 256
BLOCK = 8
DOC_DEV = 8
TOK_DEV = 1024
CAP = 640
TOKENS = 131072
DOCS = 1024
WTOK = 81920


def latin_layout(key, groups, per_pair):
    keys = jax.random.split(key, 4)
    steps = jnp.tile(jax.random.permutation(keys[0], groups), per_pair)[:DOC_DEV]
    outer = jax.random.permutation(keys[1], groups)
    inner = jax.random.permutation(keys[2], groups)
    target = outer[(inner[:, None] + steps[None, :]) % groups].astype(jnp.int32)
    local = jax.vmap(lambda k: jax.random.permutation(k, DOC_DEV))(jax.random.split(keys[3], groups)).astype(jnp.int32)
    place = local[target, jnp.arange(DOC_DEV)[None, :]].astype(jnp.int32)
    return (target, place)


def spread(key, count, top, units):
    rows = units.shape[0]
    ranks = jax.vmap(lambda k: jax.random.permutation(k, count * top))(jax.random.split(key, rows))
    taken = (ranks < units[:, None]).astype(jnp.int32)
    return jnp.sum(taken.reshape(rows, count, top), axis=2).astype(jnp.int32)


def layout(key):
    groups = DOCS // DOC_DEV
    per_pair = (DOC_DEV + groups - 1) // groups
    nblk = TOK_DEV // BLOCK
    low = (LMAX + DOC_DEV - 1 + BLOCK - 1) // BLOCK
    per_dev = CAP // BLOCK
    keys = jax.random.split(key, 6)
    units = groups * per_dev - (groups - 1) * low - nblk
    extra = spread(keys[0], groups - 1, nblk - low, jnp.full((1,), units, jnp.int32))[0]
    counts = jnp.concatenate([jnp.full((1,), nblk, jnp.int32), low + extra]).astype(jnp.int32)
    counts = counts[jax.random.permutation(keys[1], groups)].astype(jnp.int32)
    live = counts * BLOCK
    others = spread(keys[2], DOC_DEV - 1, LMAX - 1, (live - LMAX - (DOC_DEV - 1)).astype(jnp.int32))
    sized = jnp.concatenate([jnp.full((groups, 1), LMAX, jnp.int32), 1 + others], axis=1).astype(jnp.int32)
    shuffle = jax.vmap(lambda k: jax.random.permutation(k, DOC_DEV))(jax.random.split(keys[3], groups)).astype(jnp.int32)
    doc_len = jnp.take_along_axis(sized, shuffle, axis=1).astype(jnp.int32)
    ends = jnp.cumsum(doc_len, axis=1).astype(jnp.int32)
    slots = jnp.arange(TOK_DEV, dtype=jnp.int32)
    segs = jnp.sum((ends[:, None, :] <= slots[None, :, None]).astype(jnp.int32), axis=2).astype(jnp.int32)
    first_global = (jnp.cumsum(counts) - counts).astype(jnp.int32)
    blk = jnp.arange(nblk, dtype=jnp.int32)
    glob = first_global[:, None] + blk[None, :]
    dest_perm = jax.random.permutation(keys[4], groups).astype(jnp.int32)
    live_block = blk[None, :] < counts[:, None]
    dest = jnp.where(live_block, dest_perm[glob % groups], 0).astype(jnp.int32)
    row = jnp.where(live_block, glob // groups * BLOCK, CAP).astype(jnp.int32)
    plan = jnp.stack([dest, row], axis=-1).reshape(groups * nblk, 2).astype(jnp.int32)
    owner, owner_row = latin_layout(keys[5], groups, per_pair)
    corpus = (owner * DOC_DEV + owner_row).astype(jnp.int32)
    return (doc_len.reshape(DOCS), plan, corpus.reshape(DOCS), segs.reshape(TOKENS))


def draw_lengths(key, part):
    return layout(key)[0]


def draw_plan(key, part):
    return layout(key)[1]


def draw_corpus(key, part):
    return layout(key)[2]


def draw_segments(key, part):
    return layout(key)[3]


def block_levels(rng, dims, cuts, smallest, top_value):
    gain, own = 1.0, jax.random.fold_in(rng, 6)
    for dim, blocks in cuts:
        draws = jnp.exp(jax.random.uniform(jax.random.fold_in(own, dim), (blocks,), jnp.float32, smallest / len(cuts), top_value / len(cuts)))
        gain = gain * jnp.repeat(draws, dims[dim] // blocks).reshape([-1 if axis == dim else 1 for axis in range(len(dims))])
    return gain


def noise(own_key, shape, width, limit, cuts=(), kind=jnp.bfloat16):
    result = jax.random.normal(own_key, shape, jnp.float32) * width
    if len(cuts) > 0:
        result = block_levels(own_key, shape, cuts, -0.22, 0.18) * result
    return jnp.clip(result, min=-limit, max=limit).astype(kind)


def setup_inputs(seed: int = 0) -> dict:
    key_list = jax.random.split(jax.random.key(seed), 11)
    return {
        "acts": noise(key_list[0], (TOKENS, D), 1.0, 6.0, ((0, 128), (1, 2))),
        "cotangent": noise(key_list[1], (TOKENS, KV), 1.0, 6.0, ((0, 128), (1, 2))),
        "value_weight": noise(key_list[2], (KV, D), KV ** -0.5, 0.1875, ((1, 2),)),
        "proj_in": noise(key_list[3], (R, D), D ** -0.5, 0.09375, ((1, 2),)),
        "proj_out": noise(key_list[4], (R, KV), KV ** -0.5, 0.1875),
        "query_grads": noise(key_list[5], (Q, R * R), (R * R * LMAX // 4) ** -0.5, 0.01171875, ((0, 128), (1, 2))),
        "lengths": draw_lengths(jax.random.fold_in(key_list[10], 71), 0),
        "plan": draw_plan(jax.random.fold_in(key_list[10], 71), 0),
        "corpus": draw_corpus(jax.random.fold_in(key_list[10], 71), 0),
        "segments": draw_segments(jax.random.fold_in(key_list[10], 71), 0),
    }


def reference(acts, cotangent, value_weight, proj_in, proj_out, query_grads, lengths, plan, corpus, segments):
    groups = DOCS // DOC_DEV
    rank = proj_in.shape[0]
    contract = (((1,), (1,)), ((), ()))

    def per_home(items):
        acts_rows, cot_rows, seg_rows = items
        grad = jnp.dot(cot_rows, value_weight, preferred_element_type=jnp.float32).astype(jnp.bfloat16)
        in_low = lax.dot_general(acts_rows, proj_in, contract, preferred_element_type=jnp.float32).astype(jnp.bfloat16)
        out_low = lax.dot_general(cot_rows, proj_out, contract, preferred_element_type=jnp.float32).astype(jnp.bfloat16)
        member = (seg_rows[:, None] == jnp.arange(DOC_DEV, dtype=jnp.int32)[None, :]).astype(jnp.float32)
        sums = jnp.einsum("td,ta,tb->dab", member, out_low.astype(jnp.float32), in_low.astype(jnp.float32))
        return grad, jnp.concatenate([in_low, out_low], axis=1), sums.reshape(DOC_DEV, rank * rank).astype(jnp.bfloat16)

    grads, features, doc_grads = lax.map(per_home, (acts.reshape(groups, TOK_DEV, -1), cotangent.reshape(groups, TOK_DEV, -1), segments.reshape(groups, TOK_DEV)))
    input_grad = grads.reshape(TOKENS, -1)
    features = features.reshape(TOKENS, 2 * rank)
    doc_grads = doc_grads.reshape(DOCS, rank * rank)
    table = lengths.reshape(groups, DOC_DEV)
    starts = (jnp.cumsum(table, axis=1).astype(jnp.int32) - table).reshape(DOCS)
    token_ids = jnp.arange(TOKENS, dtype=jnp.int32)
    doc_ids = ((token_ids // TOK_DEV) * DOC_DEV + jnp.minimum(segments, DOC_DEV - 1)).astype(jnp.int32)
    offset = token_ids % TOK_DEV - starts[doc_ids]
    present = (segments < DOC_DEV) & (offset >= 0) & (offset < lengths[doc_ids])
    block_ids = (token_ids // BLOCK).astype(jnp.int32)
    target = jnp.where(present, plan[block_ids, 0] * CAP + plan[block_ids, 1] + token_ids % BLOCK, WTOK).astype(jnp.int32)
    balanced = jnp.zeros((WTOK, 2 * rank), jnp.bfloat16).at[target].set(features, mode="drop")
    scores = lax.dot_general(doc_grads, query_grads, contract, preferred_element_type=jnp.float32)
    influence = jnp.zeros((DOCS, Q), jnp.float32).at[corpus].set(scores)
    return input_grad, balanced, influence
```

```python
import jax
import jax.numpy as jnp
from jax import lax
from jax.experimental import pallas as pl
from jax.experimental.pallas import tpu as pltpu
from jax.sharding import PartitionSpec as P

BLOCK = 8
CAP = 640
NZ = 8
PLANE = 16
DP = 128
TOK = 1024
RANK = 64
DOCS = 8
SLOT = 16
SCORE_ROW = 8
PLACE_ROW = 12
OWNER_ROW = 13
GROUP = 4
LANES = 128
VMEM = pltpu.VMEM
F32 = jnp.float32
BF16 = jnp.bfloat16
NT = (((1,), (1,)), ((), ()))
TN = (((0,), (0,)), ((), ()))


def dot(a, b, dims=(((1,), (0,)), ((), ()))):
    return lax.dot_general(a, b, dims, preferred_element_type=F32)


def lane_iota(shape):
    return lax.broadcasted_iota(jnp.int32, shape, len(shape) - 1)


def params():
    return pltpu.CompilerParams(vmem_limit_bytes=48 * 1024 * 1024)


def partial_kernel(acts_ref, cot_ref, pin_ref, pout_ref, out_ref):
    half = cot_ref.shape[1]
    me = lax.axis_index("mp")
    pout = pout_ref[:, pl.ds(pl.multiple_of(me * half, half), half)]
    low = dot(acts_ref[...], pin_ref[...], NT)
    out = dot(cot_ref[...], pout, NT)
    out_ref[...] = jnp.concatenate([low, out], axis=1)


def partial_features(acts, cotangent, proj_in, proj_out):
    rows = 256
    return pl.pallas_call(
        partial_kernel,
        grid=(TOK // rows,),
        in_specs=[
            pl.BlockSpec((rows, acts.shape[1]), lambda i: (i, 0)),
            pl.BlockSpec((rows, cotangent.shape[1]), lambda i: (i, 0)),
            pl.BlockSpec(proj_in.shape, lambda i: (0, 0)),
            pl.BlockSpec(proj_out.shape, lambda i: (0, 0)),
        ],
        out_specs=pl.BlockSpec((rows, 2 * RANK), lambda i: (i, 0)),
        out_shape=jax.ShapeDtypeStruct((TOK, 2 * RANK), F32),
        compiler_params=params(),
        cost_estimate=pl.CostEstimate(flops=340_000_000, bytes_accessed=6_000_000, transcendentals=0),
    )(acts, cotangent, proj_in, proj_out)


def docs_kernel(own_ref, other_ref, lengths_ref, corpus_ref, feat_ref, docs_ref, scr):
    half = RANK // 2
    me = lax.axis_index("mp")
    feat = (own_ref[...] + other_ref[...]).astype(BF16)
    feat_ref[...] = feat
    row = lax.broadcasted_iota(jnp.int32, (LANES, 3 * LANES), 0)
    col = lane_iota((LANES, 3 * LANES))
    wide = col < 2 * LANES
    odd = jnp.where(col >= LANES, 1, 0)
    want = jnp.where(wide, RANK + me * half + 2 * (col % 16) + odd, col % RANK)
    pick = jnp.where(row == want, 1.0, 0.0).astype(BF16)
    spread = dot(feat, pick)
    doc = lane_iota((1, 2 * LANES)) % LANES // 16
    first = jnp.zeros((1, 2 * LANES), jnp.int32)
    last = jnp.zeros((1, 2 * LANES), jnp.int32)
    at = 0
    for i in range(DOCS):
        length = lengths_ref[i]
        first = jnp.where(doc == i, at, first)
        last = jnp.where(doc == i, at + length, last)
        at = at + length
    token = lax.broadcasted_iota(jnp.int32, (TOK, 2 * LANES), 0)
    live = (token >= first) & (token < last)
    out_cols = jnp.where(live, spread[:, : 2 * LANES], 0.0).astype(BF16)
    in_cols = spread[:, 2 * LANES :].astype(BF16)
    both = dot(out_cols, in_cols, TN)
    lane = lane_iota((LANES, LANES))
    scr[...] = jnp.where(lane < RANK, both[:LANES], both[LANES:])
    pairs = half // 2
    for p in range(pairs // 2):
        low = scr[pl.ds(p, DOCS, stride=pairs), :]
        high = scr[pl.ds(p + pairs // 2, DOCS, stride=pairs), :]
        docs_ref[:, p * LANES : (p + 1) * LANES] = jnp.concatenate([low, high], axis=0).astype(BF16)
    sub = lax.broadcasted_iota(jnp.int32, (2 * DOCS, LANES), 0)
    note = jnp.zeros((2 * DOCS, LANES), jnp.int32)
    for i in range(DOCS):
        note = jnp.where(sub == i, corpus_ref[i] // DOCS, note)
        note = jnp.where(sub == DOCS + i, corpus_ref[i] % DOCS + 1, note)
    docs_ref[:, pairs // 2 * LANES :] = note.astype(F32).astype(BF16)


def features_and_docs(own, other, lengths, corpus):
    smem = pl.BlockSpec(memory_space=pltpu.SMEM)
    vmem = pl.BlockSpec(memory_space=VMEM)
    return pl.pallas_call(
        docs_kernel,
        in_specs=[vmem, vmem, smem, smem],
        out_specs=[vmem, vmem],
        out_shape=[
            jax.ShapeDtypeStruct((TOK, 2 * RANK), BF16),
            jax.ShapeDtypeStruct((2 * DOCS, 9 * LANES), BF16),
        ],
        scratch_shapes=[VMEM((LANES, LANES), F32)],
        compiler_params=params(),
        cost_estimate=pl.CostEstimate(flops=200_000_000, bytes_accessed=1_500_000, transcendentals=0),
    )(own, other, lengths, corpus)


def score_kernel(d0, d1, d2, d3, queries_ref, out_ref):
    width = 8 * LANES
    left, right = queries_ref[:, :width], queries_ref[:, width:]
    for i, ref in enumerate((d0, d1, d2, d3)):
        piece = ref[:, :width]
        out_ref[i * DOCS : (i + 1) * DOCS, :] = (
            dot(piece, left, NT)[:DOCS] + dot(piece, right, NT)[DOCS:]
        )


def partial_scores(pieces, queries):
    vmem = pl.BlockSpec(memory_space=VMEM)
    return pl.pallas_call(
        score_kernel,
        in_specs=[vmem] * 5,
        out_specs=vmem,
        out_shape=jax.ShapeDtypeStruct((GROUP * DOCS, LANES), F32),
        compiler_params=params(),
        cost_estimate=pl.CostEstimate(flops=17_000_000, bytes_accessed=700_000, transcendentals=0),
    )(*pieces, queries)


def pack_kernel(feat_ref, plan_ref, own_ref, other_ref, d0, d1, d2, d3, out_ref, tokens, stage):
    tokens[...] = feat_ref[...].astype(F32)
    stage[...] = jnp.zeros_like(stage)
    lane = lane_iota((LANES, LANES))
    dest = plan_ref[:, 0:1]
    first = plan_ref[:, 1:2]
    send = jnp.where((dest == lane) & (first < CAP), 1.0, 0.0).astype(BF16)
    for r in range(BLOCK):
        rows = tokens[pl.ds(r, DP, stride=BLOCK), :].astype(BF16)
        stage[pl.ds(r, DP, stride=SLOT), :] = dot(send, rows, TN)
    place = jnp.broadcast_to(first // BLOCK + 1, (DP, LANES)).astype(F32).astype(BF16)
    stage[pl.ds(PLACE_ROW, DP, stride=SLOT), :] = dot(send, place, TN)
    scores = (own_ref[...] + other_ref[...]).astype(BF16).astype(F32)
    short = lane_iota((DOCS, LANES))
    marks = jnp.zeros((DP, LANES), F32)
    for i, ref in enumerate((d0, d1, d2, d3)):
        note = ref[:, 8 * LANES :].astype(F32)
        owner, row = note[:DOCS], note[DOCS:]
        hit = jnp.where(owner == short.astype(F32), 1.0, 0.0)
        stage[pl.ds(SCORE_ROW + i, DP, stride=SLOT), :] = dot(
            hit, scores[i * DOCS : (i + 1) * DOCS], TN
        )
        marks = marks + dot(hit, jnp.where(short // 32 == i, row, 0.0), TN)
    stage[pl.ds(OWNER_ROW, DP, stride=SLOT), :] = marks
    out_ref[...] = stage[...].astype(BF16)


def pack(features, plan, own, other, pieces):
    vmem = pl.BlockSpec(memory_space=VMEM)
    return pl.pallas_call(
        pack_kernel,
        in_specs=[vmem] * 8,
        out_specs=vmem,
        out_shape=jax.ShapeDtypeStruct((DP * SLOT, LANES), BF16),
        scratch_shapes=[VMEM((TOK, LANES), F32), VMEM((DP * SLOT, LANES), F32)],
        compiler_params=params(),
        cost_estimate=pl.CostEstimate(flops=40_000_000, bytes_accessed=900_000, transcendentals=0),
    )(features, plan, own, other, *pieces)


def unpack_kernel(got_ref, balanced_ref, influence_ref, stage, rows):
    stage[...] = got_ref[...].astype(F32)
    lane = lane_iota((DP, LANES))
    place = stage[pl.ds(PLACE_ROW, DP, stride=SLOT), :]
    put = jnp.where(place == (lane + 1).astype(F32), 1.0, 0.0).astype(BF16)
    for r in range(BLOCK):
        part = stage[pl.ds(r, DP, stride=SLOT), :].astype(BF16)
        rows[pl.ds(r, CAP // BLOCK, stride=BLOCK), :] = dot(put, part, TN)[: CAP // BLOCK]
    balanced_ref[...] = rows[...].astype(BF16)
    me = lax.axis_index("mp")
    count = 2 * PLANE
    short = lane_iota((count, LANES))
    want = jnp.where(short % 32 < DOCS, short % 32 + 1, -1).astype(F32)
    for j in range(2):
        base = pl.multiple_of((me * 2 + j) * count * SLOT, count * SLOT)
        mark = stage[pl.ds(base + OWNER_ROW, count, stride=SLOT), :]
        hit = jnp.where(mark == want, 1.0, 0.0).astype(BF16)
        total = jnp.zeros((DOCS, LANES), F32)
        for i in range(GROUP):
            part = stage[pl.ds(base + SCORE_ROW + i, count, stride=SLOT), :].astype(BF16)
            total = total + dot(hit, part, TN)[i * 32 : i * 32 + DOCS]
        influence_ref[:, j * LANES : (j + 1) * LANES] = total


def unpack(got):
    vmem = pl.BlockSpec(memory_space=VMEM)
    return pl.pallas_call(
        unpack_kernel,
        in_specs=[vmem],
        out_specs=[vmem, vmem],
        out_shape=[
            jax.ShapeDtypeStruct((CAP, 2 * RANK), BF16),
            jax.ShapeDtypeStruct((DOCS, 2 * LANES), F32),
        ],
        scratch_shapes=[VMEM((DP * SLOT, LANES), F32), VMEM((CAP, LANES), F32)],
        compiler_params=params(),
        cost_estimate=pl.CostEstimate(flops=40_000_000, bytes_accessed=700_000, transcendentals=0),
    )(got)


def grad_kernel(own_ref, other_ref, weight_ref, out_ref):
    half = own_ref.shape[1]
    me = lax.axis_index("mp")
    mine = weight_ref[pl.ds(pl.multiple_of(me * half, half), half), :]
    theirs = weight_ref[pl.ds(pl.multiple_of((1 - me) * half, half), half), :]
    total = dot(own_ref[...], mine) + dot(other_ref[...], theirs)
    out_ref[...] = total.astype(BF16)


def input_gradient(own, other, weight):
    rows = 256
    return pl.pallas_call(
        grad_kernel,
        grid=(TOK // rows,),
        in_specs=[
            pl.BlockSpec((rows, own.shape[1]), lambda i: (i, 0)),
            pl.BlockSpec((rows, own.shape[1]), lambda i: (i, 0)),
            pl.BlockSpec(weight.shape, lambda i: (0, 0)),
        ],
        out_specs=pl.BlockSpec((rows, weight.shape[1]), lambda i: (i, 0)),
        out_shape=jax.ShapeDtypeStruct((TOK, weight.shape[1]), BF16),
        compiler_params=params(),
        cost_estimate=pl.CostEstimate(flops=4_300_000_000, bytes_accessed=10_500_000, transcendentals=0),
    )(own, other, weight)


def body(
    acts, cotangent, value_weight, proj_in, proj_out, query_grads, lengths, plan, corpus, segments
):
    swap = [(0, 1), (1, 0)]
    pair_size = 2 * PLANE
    pairs = [[k * pair_size + i for i in range(pair_size)] for k in range(NZ // 2)]
    other_cot = lax.ppermute(cotangent, "mp", swap)
    queries = lax.all_to_all(
        jnp.broadcast_to(query_grads[None], (pair_size,) + query_grads.shape),
        "dp",
        0,
        0,
        tiled=True,
        axis_index_groups=pairs,
    ).reshape(LANES, -1)
    own = partial_features(acts, cotangent, proj_in, proj_out)
    features, docs = features_and_docs(own, lax.ppermute(own, "mp", swap), lengths, corpus)
    pieces = [docs]
    for i in range(1, GROUP):
        step = 2 * PLANE * i
        pieces.append(lax.ppermute(docs, "dp", [(s, (s + step) % DP) for s in range(DP)]))
    mine = partial_scores(pieces, queries)
    packed = pack(features, plan, mine, lax.ppermute(mine, "mp", swap), pieces)
    got = lax.all_to_all(packed.reshape(DP, SLOT, LANES), "dp", 0, 0, tiled=True)
    input_grad = input_gradient(cotangent, other_cot, value_weight)
    balanced, influence = unpack(got.reshape(DP * SLOT, LANES))
    return (input_grad, balanced, influence)


def solution(mesh):
    return jax.shard_map(
        body,
        mesh=mesh,
        in_specs=(
            P("dp", "mp"),
            P("dp", "mp"),
            P(None, "mp"),
            P(None, "mp"),
            P(),
            P("dp", "mp"),
            P("dp"),
            P("dp", None),
            P("dp"),
            P("dp"),
        ),
        out_specs=(P("dp", "mp"), P("dp", None), P("dp", "mp")),
        check_vma=False,
    )
```

```python
import jax
import jax.numpy as jnp
from jax import lax
from jax.experimental import pallas as pl
from jax.experimental.pallas import tpu as pltpu
from jax.sharding import PartitionSpec as P

BLOCK = 8
CAP = 640
DP = 128
TOK = 1024
RANK = 64
DOCS = 8
SLOT = 8
HALF_BLOCK = 4
SCORE_ROW = 4
PLACE_ROW = 6
OWNER_ROW = 7
GROUP = 4
LANES = 128
VMEM = pltpu.VMEM
F32 = jnp.float32
BF16 = jnp.bfloat16
NT = (((1,), (1,)), ((), ()))
TN = (((0,), (0,)), ((), ()))


def dot(a, b, dims=(((1,), (0,)), ((), ()))):
    return lax.dot_general(a, b, dims, preferred_element_type=F32)


def lane_iota(shape):
    return lax.broadcasted_iota(jnp.int32, shape, len(shape) - 1)


def params(mib=48):
    return pltpu.CompilerParams(vmem_limit_bytes=mib * 1024 * 1024)


def copies_kernel(source_ref, out_ref, sem):
    sends = [pltpu.make_async_copy(source_ref, out_ref.at[i], sem) for i in range(out_ref.shape[0])]
    for send in sends:
        send.start()
    for send in sends:
        send.wait()


def copies(source, count):
    return pl.pallas_call(
        copies_kernel,
        in_specs=[pl.BlockSpec(memory_space=VMEM)],
        out_specs=pl.BlockSpec(memory_space=pltpu.HBM),
        out_shape=jax.ShapeDtypeStruct((count,) + source.shape, source.dtype),
        scratch_shapes=[pltpu.SemaphoreType.DMA],
        compiler_params=params(60),
    )(source)


def partial_kernel(acts_ref, cot_ref, pin_ref, pout_ref, out_ref):
    half = cot_ref.shape[1]
    me = lax.axis_index("mp")
    pout = pout_ref[:, pl.ds(pl.multiple_of(me * half, half), half)]
    low = dot(acts_ref[...], pin_ref[...], NT)
    out = dot(cot_ref[...], pout, NT)
    out_ref[...] = jnp.concatenate([low, out], axis=1)


def partial_features(acts, cotangent, proj_in, proj_out):
    rows = 512
    return pl.pallas_call(
        partial_kernel,
        grid=(TOK // rows,),
        in_specs=[
            pl.BlockSpec((rows, acts.shape[1]), lambda i: (i, 0)),
            pl.BlockSpec((rows, cotangent.shape[1]), lambda i: (i, 0)),
            pl.BlockSpec(proj_in.shape, lambda i: (0, 0)),
            pl.BlockSpec(proj_out.shape, lambda i: (0, 0)),
        ],
        out_specs=pl.BlockSpec((rows, 2 * RANK), lambda i: (i, 0)),
        out_shape=jax.ShapeDtypeStruct((TOK, 2 * RANK), F32),
        compiler_params=params(58),
        cost_estimate=pl.CostEstimate(flops=340_000_000, bytes_accessed=6_000_000, transcendentals=0),
    )(acts, cotangent, proj_in, proj_out)


def docs_kernel(own_ref, other_ref, lengths_ref, corpus_ref, feat_ref, docs_ref, scr):
    half = RANK // 2
    me = lax.axis_index("mp")
    feat = (own_ref[...] + other_ref[...]).astype(BF16)
    feat_ref[...] = feat
    row = lax.broadcasted_iota(jnp.int32, (LANES, 3 * LANES), 0)
    col = lane_iota((LANES, 3 * LANES))
    wide = col < 2 * LANES
    odd = jnp.where(col >= LANES, 1, 0)
    want = jnp.where(wide, RANK + me * half + 2 * (col % 16) + odd, col % RANK)
    pick = jnp.where(row == want, 1.0, 0.0).astype(BF16)
    spread = dot(feat, pick)
    doc = lane_iota((1, 2 * LANES)) % LANES // 16
    first = jnp.zeros((1, 2 * LANES), jnp.int32)
    last = jnp.zeros((1, 2 * LANES), jnp.int32)
    at = 0
    for i in range(DOCS):
        length = lengths_ref[i]
        first = jnp.where(doc == i, at, first)
        last = jnp.where(doc == i, at + length, last)
        at = at + length
    token = lax.broadcasted_iota(jnp.int32, (TOK, 2 * LANES), 0)
    live = (token >= first) & (token < last)
    out_cols = jnp.where(live, spread[:, : 2 * LANES], 0.0).astype(BF16)
    in_cols = spread[:, 2 * LANES :].astype(BF16)
    both = dot(out_cols, in_cols, TN)
    lane = lane_iota((LANES, LANES))
    scr[...] = jnp.where(lane < RANK, both[:LANES], both[LANES:])
    pairs = half // 2
    for p in range(pairs // 2):
        low = scr[pl.ds(p, DOCS, stride=pairs), :]
        high = scr[pl.ds(p + pairs // 2, DOCS, stride=pairs), :]
        docs_ref[:, p * LANES : (p + 1) * LANES] = jnp.concatenate([low, high], axis=0).astype(BF16)
    sub = lax.broadcasted_iota(jnp.int32, (2 * DOCS, LANES), 0)
    note = jnp.zeros((2 * DOCS, LANES), jnp.int32)
    for i in range(DOCS):
        note = jnp.where(sub == i, corpus_ref[i] // DOCS, note)
        note = jnp.where(sub == DOCS + i, corpus_ref[i] % DOCS + 1, note)
    docs_ref[:, pairs // 2 * LANES :] = note.astype(F32).astype(BF16)


def features_and_docs(own, other, lengths, corpus):
    smem = pl.BlockSpec(memory_space=pltpu.SMEM)
    vmem = pl.BlockSpec(memory_space=VMEM)
    return pl.pallas_call(
        docs_kernel,
        in_specs=[vmem, vmem, smem, smem],
        out_specs=[vmem, vmem],
        out_shape=[
            jax.ShapeDtypeStruct((TOK, 2 * RANK), BF16),
            jax.ShapeDtypeStruct((2 * DOCS, 9 * LANES), BF16),
        ],
        scratch_shapes=[VMEM((LANES, LANES), F32)],
        compiler_params=params(),
        cost_estimate=pl.CostEstimate(flops=200_000_000, bytes_accessed=1_500_000, transcendentals=0),
    )(own, other, lengths, corpus)


def score_kernel(d0, d1, d2, d3, queries_ref, out_ref):
    width = 8 * LANES
    left, right = queries_ref[:, :width], queries_ref[:, width:]
    for i, ref in enumerate((d0, d1, d2, d3)):
        piece = ref[:, :width]
        out_ref[i * DOCS : (i + 1) * DOCS, :] = (
            dot(piece, left, NT)[:DOCS] + dot(piece, right, NT)[DOCS:]
        )


def partial_scores(pieces, queries):
    vmem = pl.BlockSpec(memory_space=VMEM)
    return pl.pallas_call(
        score_kernel,
        in_specs=[vmem] * 5,
        out_specs=vmem,
        out_shape=jax.ShapeDtypeStruct((GROUP * DOCS, LANES), F32),
        compiler_params=params(),
        cost_estimate=pl.CostEstimate(flops=17_000_000, bytes_accessed=700_000, transcendentals=0),
    )(*pieces, queries)


def place_kernel(feat_ref, plan_ref, out_ref, tokens):
    me = lax.axis_index("mp")
    tokens[...] = feat_ref[...].astype(F32)
    lane = lane_iota((DP, LANES))
    dest = plan_ref[:, 0:1]
    first = plan_ref[:, 1:2]
    send = jnp.where((dest == lane) & (first < CAP), 1.0, 0.0).astype(BF16)
    for r in range(HALF_BLOCK):
        rows = tokens[pl.ds(HALF_BLOCK * me + r, DP, stride=BLOCK), :].astype(BF16)
        out_ref[pl.ds(r, DP, stride=SLOT), :] = dot(send, rows, TN)
    for r in (SCORE_ROW, SCORE_ROW + 1, OWNER_ROW):
        out_ref[pl.ds(r, DP, stride=SLOT), :] = jnp.zeros((DP, LANES), F32)
    place = jnp.broadcast_to(first // BLOCK + 1, (DP, LANES)).astype(F32).astype(BF16)
    out_ref[pl.ds(PLACE_ROW, DP, stride=SLOT), :] = dot(send, place, TN)


def place_rows(features, plan):
    vmem = pl.BlockSpec(memory_space=VMEM)
    return pl.pallas_call(
        place_kernel,
        in_specs=[vmem] * 2,
        out_specs=vmem,
        out_shape=jax.ShapeDtypeStruct((DP * SLOT, LANES), F32),
        scratch_shapes=[VMEM((TOK, LANES), F32)],
        compiler_params=params(),
        cost_estimate=pl.CostEstimate(flops=20_000_000, bytes_accessed=900_000, transcendentals=0),
    )(features, plan)


def pack_kernel(base_ref, own_ref, other_ref, d0, d1, d2, d3, out_ref, stage):
    me = lax.axis_index("mp")
    stage[...] = base_ref[...]
    total = (own_ref[...] + other_ref[...]).astype(BF16).astype(F32)
    swapped = pltpu.roll(total, 64, 1)
    short = lane_iota(total.shape)
    piece = lax.broadcasted_iota(jnp.int32, total.shape, 0) // DOCS
    left = (short < 64) & (piece % 2 == 0)
    right = (short >= 64) & (piece % 2 == 1)
    scores = jnp.where(
        left,
        jnp.where(me == 0, total, swapped),
        jnp.where(right, jnp.where(me == 0, swapped, total), 0.0),
    ).astype(BF16)
    notes = [ref[:, 8 * LANES :].astype(F32) for ref in (d0, d1, d2, d3)]
    owner = jnp.concatenate([note[:DOCS] for note in notes], axis=0)
    row = jnp.concatenate([note[DOCS:] for note in notes], axis=0)
    hit = jnp.where(owner == short.astype(F32), 1.0, 0.0).astype(BF16)
    marks = jnp.where(short // 32 == piece, row, 0.0).astype(BF16)
    two = 2 * DOCS
    stage[pl.ds(SCORE_ROW, DP, stride=SLOT), :] = dot(hit[:two], scores[:two], TN)
    stage[pl.ds(SCORE_ROW + 1, DP, stride=SLOT), :] = dot(hit[two:], scores[two:], TN)
    stage[pl.ds(OWNER_ROW, DP, stride=SLOT), :] = dot(hit, marks, TN)
    out_ref[...] = stage[...].astype(BF16)


def pack(base, own, other, pieces):
    vmem = pl.BlockSpec(memory_space=VMEM)
    return pl.pallas_call(
        pack_kernel,
        in_specs=[vmem] * 7,
        out_specs=vmem,
        out_shape=jax.ShapeDtypeStruct((DP * SLOT, LANES), BF16),
        scratch_shapes=[VMEM((DP * SLOT, LANES), F32)],
        compiler_params=params(),
        cost_estimate=pl.CostEstimate(flops=4_000_000, bytes_accessed=900_000, transcendentals=0),
    )(base, own, other, *pieces)


def split_kernel(got_ref, after_ref, rows_ref, notes_ref, stage):
    stage[...] = got_ref[...].astype(F32)
    for r in range(HALF_BLOCK):
        part = stage[pl.ds(r, DP, stride=SLOT), :]
        rows_ref[r * DP : (r + 1) * DP, :] = part.astype(BF16)
    for r in range(HALF_BLOCK, SLOT):
        part = stage[pl.ds(r, DP, stride=SLOT), :]
        notes_ref[(r - HALF_BLOCK) * DP : (r - HALF_BLOCK + 1) * DP, :] = part


def split(got, after):
    vmem = pl.BlockSpec(memory_space=VMEM)
    return pl.pallas_call(
        split_kernel,
        in_specs=[vmem, pl.BlockSpec(memory_space=pl.ANY)],
        out_specs=[vmem, vmem],
        out_shape=[
            jax.ShapeDtypeStruct((HALF_BLOCK * DP, LANES), BF16),
            jax.ShapeDtypeStruct((HALF_BLOCK * DP, LANES), F32),
        ],
        scratch_shapes=[VMEM((DP * SLOT, LANES), F32)],
        compiler_params=params(),
        cost_estimate=pl.CostEstimate(flops=0, bytes_accessed=600_000, transcendentals=0),
    )(got, after)


def influence_kernel(notes_ref, influence_ref):
    count = DP // GROUP
    short = lane_iota((count, LANES))
    want = jnp.where(short % 32 < DOCS, short % 32 + 1, -1).astype(F32)
    low = lane_iota((DOCS, LANES)) < 64
    parts = []
    for x in range(GROUP):

        def taken(row):
            return notes_ref[pl.ds((row - HALF_BLOCK) * DP + x, count, stride=GROUP), :]

        hit = jnp.where(taken(OWNER_ROW) == want, 1.0, 0.0).astype(BF16)
        one = dot(hit, taken(SCORE_ROW).astype(BF16), TN)
        two = dot(hit, taken(SCORE_ROW + 1).astype(BF16), TN)
        parts.append(
            jnp.where(low, one[0:8] + two[64:72], one[32:40] + two[96:104]).astype(BF16)
        )
    source = lax.broadcasted_iota(jnp.int32, (GROUP * LANES, 2 * LANES), 0)
    column = lane_iota((GROUP * LANES, 2 * LANES))
    target = source % 64 // 4 * 16 + source // LANES * 4 + source % 4
    order = jnp.where(column == target, 1.0, 0.0).astype(BF16)
    influence_ref[...] = dot(jnp.concatenate(parts, axis=1), order)


def influence_rows(notes):
    vmem = pl.BlockSpec(memory_space=VMEM)
    return pl.pallas_call(
        influence_kernel,
        in_specs=[vmem],
        out_specs=vmem,
        out_shape=jax.ShapeDtypeStruct((DOCS, 2 * LANES), F32),
        compiler_params=params(),
        cost_estimate=pl.CostEstimate(flops=2_000_000, bytes_accessed=270_000, transcendentals=0),
    )(notes)


def balance_kernel(own_ref, other_ref, notes_ref, balanced_ref, rows):
    me = lax.axis_index("mp")
    lane = lane_iota((DP, LANES))
    place = notes_ref[(PLACE_ROW - HALF_BLOCK) * DP : (PLACE_ROW - HALF_BLOCK + 1) * DP, :]
    put = jnp.where(place == (lane + 1).astype(F32), 1.0, 0.0).astype(BF16)
    blocks = CAP // BLOCK
    for r in range(HALF_BLOCK):
        near = own_ref[r * DP : (r + 1) * DP, :]
        far = other_ref[r * DP : (r + 1) * DP, :]
        rows[pl.ds(HALF_BLOCK * me + r, blocks, stride=BLOCK), :] = dot(put, near, TN)[:blocks]
        rows[pl.ds(HALF_BLOCK * (1 - me) + r, blocks, stride=BLOCK), :] = dot(put, far, TN)[:blocks]
    balanced_ref[...] = rows[...].astype(BF16)


def balance(own, other, notes):
    vmem = pl.BlockSpec(memory_space=VMEM)
    return pl.pallas_call(
        balance_kernel,
        in_specs=[vmem, vmem, vmem],
        out_specs=vmem,
        out_shape=jax.ShapeDtypeStruct((CAP, 2 * RANK), BF16),
        scratch_shapes=[VMEM((CAP, LANES), F32)],
        compiler_params=params(),
        cost_estimate=pl.CostEstimate(flops=40_000_000, bytes_accessed=700_000, transcendentals=0),
    )(own, other, notes)


def grad_kernel(own_ref, other_ref, weight_ref, out_ref, token_ref):
    token_ref[...] = jnp.zeros_like(token_ref)
    half = own_ref.shape[1]
    me = lax.axis_index("mp")
    mine = weight_ref[pl.ds(pl.multiple_of(me * half, half), half), :]
    theirs = weight_ref[pl.ds(pl.multiple_of((1 - me) * half, half), half), :]
    total = dot(own_ref[...], mine) + dot(other_ref[...], theirs)
    out_ref[...] = total.astype(BF16)


def input_gradient(own, other, weight):
    rows = 256
    return pl.pallas_call(
        grad_kernel,
        grid=(TOK // rows,),
        in_specs=[
            pl.BlockSpec((rows, own.shape[1]), lambda i: (i, 0)),
            pl.BlockSpec((rows, own.shape[1]), lambda i: (i, 0)),
            pl.BlockSpec(weight.shape, lambda i: (0, 0)),
        ],
        out_specs=[
            pl.BlockSpec((rows, weight.shape[1]), lambda i: (i, 0)),
            pl.BlockSpec((8, LANES), lambda i: (0, 0)),
        ],
        out_shape=[
            jax.ShapeDtypeStruct((TOK, weight.shape[1]), BF16),
            jax.ShapeDtypeStruct((8, LANES), F32),
        ],
        compiler_params=params(),
        cost_estimate=pl.CostEstimate(flops=4_300_000_000, bytes_accessed=10_500_000, transcendentals=0),
    )(own, other, weight)


def body(
    acts, cotangent, value_weight, proj_in, proj_out, query_grads, lengths, plan, corpus, segments
):
    swap = [(0, 1), (1, 0)]
    members = DP // GROUP
    columns = [[k + GROUP * i for i in range(members)] for k in range(GROUP)]
    other_cot = lax.ppermute(cotangent, "mp", swap)
    queries = lax.all_to_all(
        copies(query_grads, members),
        "dp",
        0,
        0,
        tiled=True,
        axis_index_groups=columns,
    ).reshape(LANES, -1)
    own = partial_features(acts, cotangent, proj_in, proj_out)
    features, docs = features_and_docs(own, lax.ppermute(own, "mp", swap), lengths, corpus)
    pieces = [docs]
    for i in range(1, GROUP):
        row = [(s, s - s % GROUP + (s + i) % GROUP) for s in range(DP)]
        pieces.append(lax.ppermute(docs, "dp", row))
    mine = partial_scores(pieces, queries)
    packed = pack(place_rows(features, plan), mine, lax.ppermute(mine, "mp", swap), pieces)
    got = lax.all_to_all(packed.reshape(DP, SLOT, LANES), "dp", 0, 0, tiled=True)
    input_grad, token = input_gradient(cotangent, other_cot, value_weight)
    rows, notes = split(got.reshape(DP * SLOT, LANES), token)
    balanced = balance(rows, lax.ppermute(rows, "mp", swap), notes)
    influence = influence_rows(notes)
    return (input_grad, balanced, influence)


def solution(mesh):
    return jax.shard_map(
        body,
        mesh=mesh,
        in_specs=(
            P("dp", "mp"),
            P("dp", "mp"),
            P(None, "mp"),
            P(None, "mp"),
            P(),
            P("dp", "mp"),
            P("dp"),
            P("dp", None),
            P("dp"),
            P("dp"),
        ),
        out_specs=(P("dp", "mp"), P("dp", None), P("dp", "mp")),
        check_vma=False,
    )
```

```python
import jax
import jax.numpy as jnp
from jax import lax
from jax.experimental import pallas as pl
from jax.experimental.pallas import tpu as pltpu
from jax.sharding import PartitionSpec as P

BLOCK = 8
CAP = 640
DP = 128
TOK = 1024
RANK = 64
DOCS = 8
SLOT = 8
HALF_BLOCK = 4
SCORE_ROW = 4
PLACE_ROW = 6
OWNER_ROW = 7
GROUP = 4
CHUNKS = ((0, 256), (256, 256), (512, 256), (768, 256))
LANES = 128
VMEM = pltpu.VMEM
F32 = jnp.float32
BF16 = jnp.bfloat16
NT = (((1,), (1,)), ((), ()))
TN = (((0,), (0,)), ((), ()))


def dot(a, b, dims=(((1,), (0,)), ((), ()))):
    return lax.dot_general(a, b, dims, preferred_element_type=F32)


def lane_iota(shape):
    return lax.broadcasted_iota(jnp.int32, shape, len(shape) - 1)


def params(mib=48):
    return pltpu.CompilerParams(vmem_limit_bytes=mib * 1024 * 1024)


def copies_kernel(source_ref, out_ref, held, sem, out_sem):
    load = pltpu.make_async_copy(source_ref, held, sem)
    load.start()
    load.wait()
    sends = [pltpu.make_async_copy(held, out_ref.at[i], out_sem) for i in range(out_ref.shape[0])]
    for send in sends:
        send.start()
    for send in sends:
        send.wait()


def copies(source, count):
    hbm = pl.BlockSpec(memory_space=pl.ANY)
    return pl.pallas_call(
        copies_kernel,
        in_specs=[hbm],
        out_specs=hbm,
        out_shape=pltpu.HBM((count,) + source.shape, source.dtype),
        scratch_shapes=[
            VMEM(source.shape, source.dtype),
            pltpu.SemaphoreType.DMA,
            pltpu.SemaphoreType.DMA,
        ],
        compiler_params=params(4),
    )(pltpu.with_memory_space_constraint(source, pltpu.HBM))


def partial_kernel(
    acts_ref, cot_ref, pin_ref, pout_ref, out_ref, acts, cot, pin, pout, in_sems
):
    half = cot_ref.shape[1]
    me = lax.axis_index("mp")
    weights = [
        pltpu.make_async_copy(pin_ref, pin, in_sems.at[0]),
        pltpu.make_async_copy(
            pout_ref.at[:, pl.ds(pl.multiple_of(me * half, half), half)], pout, in_sems.at[1]
        ),
    ]
    loads = []
    for i, (at, rows) in enumerate(CHUNKS):
        span = pl.ds(at, rows)
        loads.append(
            [
                pltpu.make_async_copy(acts_ref.at[span], acts.at[span], in_sems.at[2 + 2 * i]),
                pltpu.make_async_copy(cot_ref.at[span], cot.at[span], in_sems.at[3 + 2 * i]),
            ]
        )
    for copy in weights + loads[0] + loads[1]:
        copy.start()
    for copy in weights:
        copy.wait()
    for i, (at, rows) in enumerate(CHUNKS):
        span = pl.ds(at, rows)
        for copy in loads[i]:
            copy.wait()
        if i + 2 < len(CHUNKS):
            for copy in loads[i + 2]:
                copy.start()
        low = dot(acts[span, :], pin[...], NT)
        high = dot(cot[span, :], pout[...], NT)
        out_ref[span, :] = jnp.concatenate([low, high], axis=1)


def partial_features(acts, cotangent, proj_in, proj_out):
    hbm = pl.BlockSpec(memory_space=pl.ANY)
    half = cotangent.shape[1]
    return pl.pallas_call(
        partial_kernel,
        in_specs=[hbm] * 4,
        out_specs=pl.BlockSpec(memory_space=VMEM),
        out_shape=VMEM((TOK, 2 * RANK), F32),
        scratch_shapes=[
            VMEM(acts.shape, BF16),
            VMEM(cotangent.shape, BF16),
            VMEM(proj_in.shape, BF16),
            VMEM((RANK, half), BF16),
            pltpu.SemaphoreType.DMA((2 + 2 * len(CHUNKS),)),
        ],
        compiler_params=params(16),
        cost_estimate=pl.CostEstimate(flops=340_000_000, bytes_accessed=6_000_000, transcendentals=0),
    )(*(pltpu.with_memory_space_constraint(x, pltpu.HBM) for x in (acts, cotangent, proj_in, proj_out)))


def docs_kernel(own_ref, other_ref, lengths_ref, corpus_ref, feat_ref, docs_ref, scr):
    half = RANK // 2
    me = lax.axis_index("mp")
    feat = (own_ref[...].astype(F32) + other_ref[...].astype(F32)).astype(BF16)
    feat_ref[...] = feat
    row = lax.broadcasted_iota(jnp.int32, (LANES, 3 * LANES), 0)
    col = lane_iota((LANES, 3 * LANES))
    wide = col < 2 * LANES
    odd = jnp.where(col >= LANES, 1, 0)
    want = jnp.where(wide, RANK + me * half + 2 * (col % 16) + odd, col % RANK)
    pick = jnp.where(row == want, 1.0, 0.0).astype(BF16)
    spread = dot(feat, pick)
    doc = lane_iota((1, 2 * LANES)) % LANES // 16
    first = jnp.zeros((1, 2 * LANES), jnp.int32)
    last = jnp.zeros((1, 2 * LANES), jnp.int32)
    at = 0
    for i in range(DOCS):
        length = lengths_ref[i]
        first = jnp.where(doc == i, at, first)
        last = jnp.where(doc == i, at + length, last)
        at = at + length
    token = lax.broadcasted_iota(jnp.int32, (TOK, 2 * LANES), 0)
    live = (token >= first) & (token < last)
    out_cols = jnp.where(live, spread[:, : 2 * LANES], 0.0).astype(BF16)
    in_cols = spread[:, 2 * LANES :].astype(BF16)
    both = dot(out_cols, in_cols, TN)
    lane = lane_iota((LANES, LANES))
    scr[...] = jnp.where(lane < RANK, both[:LANES], both[LANES:])
    pairs = half // 2
    for p in range(pairs // 2):
        low = scr[pl.ds(p, DOCS, stride=pairs), :]
        high = scr[pl.ds(p + pairs // 2, DOCS, stride=pairs), :]
        docs_ref[:, p * LANES : (p + 1) * LANES] = jnp.concatenate([low, high], axis=0).astype(BF16)
    sub = lax.broadcasted_iota(jnp.int32, (2 * DOCS, LANES), 0)
    note = jnp.zeros((2 * DOCS, LANES), jnp.int32)
    for i in range(DOCS):
        note = jnp.where(sub == i, corpus_ref[i] // DOCS, note)
        note = jnp.where(sub == DOCS + i, corpus_ref[i] % DOCS + 1, note)
    docs_ref[:, pairs // 2 * LANES :] = note.astype(F32).astype(BF16)


def features_and_docs(own, other, lengths, corpus):
    smem = pl.BlockSpec(memory_space=pltpu.SMEM)
    vmem = pl.BlockSpec(memory_space=VMEM)
    return pl.pallas_call(
        docs_kernel,
        in_specs=[vmem, vmem, smem, smem],
        out_specs=[vmem, vmem],
        out_shape=[
            jax.ShapeDtypeStruct((TOK, 2 * RANK), BF16),
            jax.ShapeDtypeStruct((2 * DOCS, 9 * LANES), BF16),
        ],
        scratch_shapes=[VMEM((LANES, LANES), F32)],
        compiler_params=params(),
        cost_estimate=pl.CostEstimate(flops=200_000_000, bytes_accessed=1_500_000, transcendentals=0),
    )(own, other, lengths, corpus)


def score_kernel(d0, d1, d2, d3, queries_ref, out_ref):
    width = 8 * LANES
    rows = queries_ref[...].reshape(LANES, 2 * width)
    left, right = rows[:, :width], rows[:, width:]
    for i, ref in enumerate((d0, d1, d2, d3)):
        piece = ref[:, :width]
        out_ref[i * DOCS : (i + 1) * DOCS, :] = (
            dot(piece, left, NT)[:DOCS] + dot(piece, right, NT)[DOCS:]
        )


def partial_scores(pieces, queries):
    vmem = pl.BlockSpec(memory_space=VMEM)
    return pl.pallas_call(
        score_kernel,
        in_specs=[vmem] * 5,
        out_specs=vmem,
        out_shape=jax.ShapeDtypeStruct((GROUP * DOCS, LANES), F32),
        compiler_params=params(),
        cost_estimate=pl.CostEstimate(flops=17_000_000, bytes_accessed=700_000, transcendentals=0),
    )(*pieces, queries)


def place_kernel(feat_ref, plan_ref, out_ref, tokens):
    me = lax.axis_index("mp")
    tokens[...] = feat_ref[...].astype(F32)
    lane = lane_iota((DP, LANES))
    dest = plan_ref[:, 0:1]
    first = plan_ref[:, 1:2]
    send = jnp.where((dest == DP - 1 - lane) & (first < CAP), 1.0, 0.0).astype(BF16)
    for r in range(HALF_BLOCK):
        rows = tokens[pl.ds(HALF_BLOCK * me + r, DP, stride=BLOCK), :].astype(BF16)
        out_ref[pl.ds(r, DP, stride=SLOT), :] = dot(send, rows, TN)
    for r in (SCORE_ROW, SCORE_ROW + 1, OWNER_ROW):
        out_ref[pl.ds(r, DP, stride=SLOT), :] = jnp.zeros((DP, LANES), F32)
    place = jnp.broadcast_to(first // BLOCK + 1, (DP, LANES)).astype(F32).astype(BF16)
    out_ref[pl.ds(PLACE_ROW, DP, stride=SLOT), :] = dot(send, place, TN)


def place_rows(features, plan):
    vmem = pl.BlockSpec(memory_space=VMEM)
    return pl.pallas_call(
        place_kernel,
        in_specs=[vmem] * 2,
        out_specs=vmem,
        out_shape=jax.ShapeDtypeStruct((DP * SLOT, LANES), F32),
        scratch_shapes=[VMEM((TOK, LANES), F32)],
        compiler_params=params(),
        cost_estimate=pl.CostEstimate(flops=20_000_000, bytes_accessed=900_000, transcendentals=0),
    )(features, plan)


def pack_kernel(base_ref, own_ref, other_ref, d0, d1, d2, d3, out_ref, stage):
    me = lax.axis_index("mp")
    stage[...] = base_ref[...]
    total = (own_ref[...] + other_ref[...]).astype(BF16).astype(F32)
    swapped = pltpu.roll(total, 64, 1)
    short = lane_iota(total.shape)
    piece = lax.broadcasted_iota(jnp.int32, total.shape, 0) // DOCS
    left = (short < 64) & (piece % 2 == 0)
    right = (short >= 64) & (piece % 2 == 1)
    scores = jnp.where(
        left,
        jnp.where(me == 0, total, swapped),
        jnp.where(right, jnp.where(me == 0, swapped, total), 0.0),
    ).astype(BF16)
    notes = [ref[:, 8 * LANES :].astype(F32) for ref in (d0, d1, d2, d3)]
    owner = jnp.concatenate([note[:DOCS] for note in notes], axis=0)
    row = jnp.concatenate([note[DOCS:] for note in notes], axis=0)
    hit = jnp.where(owner == (DP - 1 - short).astype(F32), 1.0, 0.0).astype(BF16)
    marks = jnp.where(short // 32 == piece, row, 0.0).astype(BF16)
    two = 2 * DOCS
    stage[pl.ds(SCORE_ROW, DP, stride=SLOT), :] = dot(hit[:two], scores[:two], TN)
    stage[pl.ds(SCORE_ROW + 1, DP, stride=SLOT), :] = dot(hit[two:], scores[two:], TN)
    stage[pl.ds(OWNER_ROW, DP, stride=SLOT), :] = dot(hit, marks, TN)
    out_ref[...] = stage[...].astype(BF16)


def pack(base, own, other, pieces):
    vmem = pl.BlockSpec(memory_space=VMEM)
    return pl.pallas_call(
        pack_kernel,
        in_specs=[vmem] * 7,
        out_specs=vmem,
        out_shape=jax.ShapeDtypeStruct((DP * SLOT, LANES), BF16),
        scratch_shapes=[VMEM((DP * SLOT, LANES), F32)],
        compiler_params=params(),
        cost_estimate=pl.CostEstimate(flops=4_000_000, bytes_accessed=900_000, transcendentals=0),
    )(base, own, other, *pieces)


def split_kernel(got_ref, after_ref, rows_ref, notes_ref, stage):
    stage[...] = got_ref[...].astype(F32)
    for r in range(HALF_BLOCK):
        part = stage[pl.ds(r, DP, stride=SLOT), :]
        rows_ref[r * DP : (r + 1) * DP, :] = part.astype(BF16)
    for r in range(HALF_BLOCK, SLOT):
        part = stage[pl.ds(r, DP, stride=SLOT), :]
        notes_ref[(r - HALF_BLOCK) * DP : (r - HALF_BLOCK + 1) * DP, :] = part


def split(got, after):
    vmem = pl.BlockSpec(memory_space=VMEM)
    return pl.pallas_call(
        split_kernel,
        in_specs=[vmem, pl.BlockSpec(memory_space=pl.ANY)],
        out_specs=[vmem, vmem],
        out_shape=[
            jax.ShapeDtypeStruct((HALF_BLOCK * DP, LANES), BF16),
            jax.ShapeDtypeStruct((HALF_BLOCK * DP, LANES), F32),
        ],
        scratch_shapes=[VMEM((DP * SLOT, LANES), F32)],
        compiler_params=params(),
        cost_estimate=pl.CostEstimate(flops=0, bytes_accessed=600_000, transcendentals=0),
    )(got, after)


def influence_kernel(notes_ref, influence_ref):
    count = DP // GROUP
    short = lane_iota((count, LANES))
    want = jnp.where(short % 32 < DOCS, short % 32 + 1, -1).astype(F32)
    low = lane_iota((DOCS, LANES)) < 64
    parts = []
    for x in range(GROUP):

        def taken(row):
            return notes_ref[pl.ds((row - HALF_BLOCK) * DP + x, count, stride=GROUP), :]

        hit = jnp.where(taken(OWNER_ROW) == want, 1.0, 0.0).astype(BF16)
        one = dot(hit, taken(SCORE_ROW).astype(BF16), TN)
        two = dot(hit, taken(SCORE_ROW + 1).astype(BF16), TN)
        parts.append(
            jnp.where(low, one[0:8] + two[64:72], one[32:40] + two[96:104]).astype(BF16)
        )
    source = lax.broadcasted_iota(jnp.int32, (GROUP * LANES, 2 * LANES), 0)
    column = lane_iota((GROUP * LANES, 2 * LANES))
    target = source % 64 // 4 * 16 + (GROUP - 1 - source // LANES) * 4 + source % 4
    order = jnp.where(column == target, 1.0, 0.0).astype(BF16)
    influence_ref[...] = dot(jnp.concatenate(parts, axis=1), order)


def influence_rows(notes):
    vmem = pl.BlockSpec(memory_space=VMEM)
    return pl.pallas_call(
        influence_kernel,
        in_specs=[vmem],
        out_specs=vmem,
        out_shape=jax.ShapeDtypeStruct((DOCS, 2 * LANES), F32),
        compiler_params=params(),
        cost_estimate=pl.CostEstimate(flops=2_000_000, bytes_accessed=270_000, transcendentals=0),
    )(notes)


def balance_kernel(own_ref, other_ref, notes_ref, balanced_ref, rows):
    me = lax.axis_index("mp")
    lane = lane_iota((DP, LANES))
    place = notes_ref[(PLACE_ROW - HALF_BLOCK) * DP : (PLACE_ROW - HALF_BLOCK + 1) * DP, :]
    put = jnp.where(place == (lane + 1).astype(F32), 1.0, 0.0).astype(BF16)
    blocks = CAP // BLOCK
    for r in range(HALF_BLOCK):
        near = own_ref[r * DP : (r + 1) * DP, :]
        far = other_ref[r * DP : (r + 1) * DP, :]
        rows[pl.ds(HALF_BLOCK * me + r, blocks, stride=BLOCK), :] = dot(put, near, TN)[:blocks]
        rows[pl.ds(HALF_BLOCK * (1 - me) + r, blocks, stride=BLOCK), :] = dot(put, far, TN)[:blocks]
    balanced_ref[...] = rows[...].astype(BF16)


def balance(own, other, notes):
    vmem = pl.BlockSpec(memory_space=VMEM)
    return pl.pallas_call(
        balance_kernel,
        in_specs=[vmem, vmem, vmem],
        out_specs=vmem,
        out_shape=jax.ShapeDtypeStruct((CAP, 2 * RANK), BF16),
        scratch_shapes=[VMEM((CAP, LANES), F32)],
        compiler_params=params(),
        cost_estimate=pl.CostEstimate(flops=40_000_000, bytes_accessed=700_000, transcendentals=0),
    )(own, other, notes)


def grad_kernel(own_ref, other_ref, weight_ref, out_ref, token_ref):
    half = own_ref.shape[1]
    me = lax.axis_index("mp")
    mine = weight_ref[pl.ds(pl.multiple_of(me * half, half), half), :]
    theirs = weight_ref[pl.ds(pl.multiple_of((1 - me) * half, half), half), :]
    total = dot(own_ref[...], mine) + dot(other_ref[...], theirs)
    out_ref[...] = total.astype(BF16)
    token_ref[...] = jnp.zeros_like(token_ref)


def input_gradient(own, other, weight):
    columns = 512
    return pl.pallas_call(
        grad_kernel,
        grid=(weight.shape[1] // columns,),
        in_specs=[
            pl.BlockSpec(own.shape, lambda j: (0, 0)),
            pl.BlockSpec(other.shape, lambda j: (0, 0)),
            pl.BlockSpec((weight.shape[0], columns), lambda j: (0, j)),
        ],
        out_specs=[
            pl.BlockSpec((TOK, columns), lambda j: (0, j)),
            pl.BlockSpec((8, LANES), lambda j: (0, 0)),
        ],
        out_shape=[
            jax.ShapeDtypeStruct((TOK, weight.shape[1]), BF16),
            jax.ShapeDtypeStruct((8, LANES), F32),
        ],
        compiler_params=params(),
        cost_estimate=pl.CostEstimate(flops=4_300_000_000, bytes_accessed=10_500_000, transcendentals=0),
    )(own, other, weight)


def body(
    acts, cotangent, value_weight, proj_in, proj_out, query_grads, lengths, plan, corpus, segments
):
    swap = [(0, 1), (1, 0)]
    members = DP // GROUP
    columns = [[k + GROUP * i for i in range(members)] for k in range(GROUP)]
    other_cot = lax.ppermute(cotangent, "mp", swap)
    queries = lax.all_to_all(
        copies(query_grads, members),
        "dp",
        0,
        0,
        tiled=True,
        axis_index_groups=columns,
    )
    own = partial_features(acts, cotangent, proj_in, proj_out)
    features, docs = features_and_docs(own, lax.ppermute(own, "mp", swap), lengths, corpus)
    pieces = [docs]
    for i in range(1, GROUP):
        pieces.append(lax.ppermute(docs, "dp", [(s, s ^ i) for s in range(DP)]))
    mine = partial_scores(pieces, queries)
    packed = pack(place_rows(features, plan), mine, lax.ppermute(mine, "mp", swap), pieces)
    got = lax.all_to_all(
        packed.reshape(DP, SLOT, LANES),
        "dp",
        0,
        0,
        tiled=True,
        axis_index_groups=[list(range(DP - 1, -1, -1))],
    )
    input_grad, token = input_gradient(cotangent, other_cot, value_weight)
    rows, notes = split(got.reshape(DP * SLOT, LANES), token)
    balanced = balance(rows, lax.ppermute(rows, "mp", swap), notes)
    influence = influence_rows(notes)
    return (input_grad, balanced, influence)


def solution(mesh):
    return jax.shard_map(
        body,
        mesh=mesh,
        in_specs=(
            P("dp", "mp"),
            P("dp", "mp"),
            P(None, "mp"),
            P(None, "mp"),
            P(),
            P("dp", "mp"),
            P("dp"),
            P("dp", None),
            P("dp"),
            P("dp"),
        ),
        out_specs=(P("dp", "mp"), P("dp", None), P("dp", "mp")),
        check_vma=False,
    )
```

```python
import jax
import jax.numpy as jnp
from jax import lax
from jax.experimental import pallas as pl
from jax.experimental.pallas import tpu as pltpu
from jax.sharding import PartitionSpec as P

BLOCK = 8
CAP = 640
DP = 128
TOK = 1024
RANK = 64
DOCS = 8
SLOT = 8
HALF_BLOCK = 4
SCORE_ROW = 4
PLACE_ROW = 6
OWNER_ROW = 7
GROUP = 4
PAD = 8
CHUNKS = ((0, 256), (256, 256), (512, 256), (768, 256))
LANES = 128
VMEM = pltpu.VMEM
F32 = jnp.float32
BF16 = jnp.bfloat16
NT = (((1,), (1,)), ((), ()))
TN = (((0,), (0,)), ((), ()))


def dot(a, b, dims=(((1,), (0,)), ((), ()))):
    return lax.dot_general(a, b, dims, preferred_element_type=F32)


def slot_of(device):
    z, y, x = device // 16, device // GROUP % GROUP, device % GROUP
    return DP - 1 - (x * 32 + y * 8 + z)


def lane_iota(shape):
    return lax.broadcasted_iota(jnp.int32, shape, len(shape) - 1)


def params(mib=48):
    return pltpu.CompilerParams(vmem_limit_bytes=mib * 1024 * 1024)


def copies_kernel(source_ref, out_ref, held, sem, out_sem):
    load = pltpu.make_async_copy(source_ref, held, sem)
    load.start()
    load.wait()
    sends = [pltpu.make_async_copy(held, out_ref.at[i], out_sem) for i in range(out_ref.shape[0])]
    for send in sends:
        send.start()
    for send in sends:
        send.wait()


def copies(source, count):
    hbm = pl.BlockSpec(memory_space=pl.ANY)
    return pl.pallas_call(
        copies_kernel,
        in_specs=[hbm],
        out_specs=hbm,
        out_shape=pltpu.HBM((count,) + source.shape, source.dtype),
        scratch_shapes=[
            VMEM(source.shape, source.dtype),
            pltpu.SemaphoreType.DMA,
            pltpu.SemaphoreType.DMA,
        ],
        compiler_params=params(4),
    )(pltpu.with_memory_space_constraint(source, pltpu.HBM))


def partial_kernel(
    acts_ref, cot_ref, pin_ref, pout_ref, out_ref, acts, cot, pin, pout, in_sems
):
    half = cot_ref.shape[1]
    me = lax.axis_index("mp")
    weights = [
        pltpu.make_async_copy(pin_ref, pin, in_sems.at[0]),
        pltpu.make_async_copy(
            pout_ref.at[:, pl.ds(pl.multiple_of(me * half, half), half)], pout, in_sems.at[1]
        ),
    ]
    loads = []
    for i, (at, rows) in enumerate(CHUNKS):
        span = pl.ds(at, rows)
        loads.append(
            [
                pltpu.make_async_copy(acts_ref.at[span], acts.at[span], in_sems.at[2 + 2 * i]),
                pltpu.make_async_copy(cot_ref.at[span], cot.at[span], in_sems.at[3 + 2 * i]),
            ]
        )
    for copy in weights + loads[0] + loads[1]:
        copy.start()
    for copy in weights:
        copy.wait()
    for i, (at, rows) in enumerate(CHUNKS):
        span = pl.ds(at, rows)
        for copy in loads[i]:
            copy.wait()
        if i + 2 < len(CHUNKS):
            for copy in loads[i + 2]:
                copy.start()
        low = dot(acts[span, :], pin[...], NT)
        high = dot(cot[span, :], pout[...], NT)
        out_ref[span, :] = jnp.concatenate([low, high], axis=1)


def partial_features(acts, cotangent, proj_in, proj_out):
    hbm = pl.BlockSpec(memory_space=pl.ANY)
    half = cotangent.shape[1]
    return pl.pallas_call(
        partial_kernel,
        in_specs=[hbm] * 4,
        out_specs=pl.BlockSpec(memory_space=VMEM),
        out_shape=VMEM((TOK, 2 * RANK), F32),
        scratch_shapes=[
            VMEM(acts.shape, BF16),
            VMEM(cotangent.shape, BF16),
            VMEM(proj_in.shape, BF16),
            VMEM((RANK, half), BF16),
            pltpu.SemaphoreType.DMA((2 + 2 * len(CHUNKS),)),
        ],
        compiler_params=params(16),
        cost_estimate=pl.CostEstimate(flops=340_000_000, bytes_accessed=6_000_000, transcendentals=0),
    )(*(pltpu.with_memory_space_constraint(x, pltpu.HBM) for x in (acts, cotangent, proj_in, proj_out)))


def docs_kernel(own_ref, other_ref, lengths_ref, corpus_ref, feat_ref, docs_ref, scr):
    half = RANK // 2
    me = lax.axis_index("mp")
    feat = (own_ref[...].astype(F32) + other_ref[...].astype(F32)).astype(BF16)
    feat_ref[...] = feat
    wide = 2 * LANES
    row = lax.broadcasted_iota(jnp.int32, (wide, LANES), 0)
    want = RANK + me * half + 2 * (row % 16) + row // LANES
    pick = jnp.where(lane_iota((wide, LANES)) == want, 1.0, 0.0).astype(BF16)
    spread = dot(pick, feat, NT)
    doc = lax.broadcasted_iota(jnp.int32, (wide, 1), 0) % LANES // 16
    first = jnp.zeros((wide, 1), jnp.int32)
    last = jnp.zeros((wide, 1), jnp.int32)
    at = 0
    for i in range(DOCS):
        length = lengths_ref[i]
        first = jnp.where(doc == i, at, first)
        last = jnp.where(doc == i, at + length, last)
        at = at + length
    token = lane_iota((wide, TOK))
    live = (token >= first) & (token < last)
    both = dot(jnp.where(live, spread, 0.0).astype(BF16), feat)
    left = lane_iota((LANES, LANES)) < RANK
    scr[0:LANES, :] = jnp.where(left, both[:LANES], pltpu.roll(both[LANES:], RANK, 1))
    pairs = half // 2
    for p in range(pairs // 2):
        low = scr[pl.ds(p, DOCS, stride=pairs), :]
        high = scr[pl.ds(p + pairs // 2, DOCS, stride=pairs), :]
        docs_ref[:, p * LANES : (p + 1) * LANES] = jnp.concatenate([low, high], axis=0).astype(BF16)
    sub = lax.broadcasted_iota(jnp.int32, (2 * DOCS, LANES), 0)
    note = jnp.zeros((2 * DOCS, LANES), jnp.int32)
    for i in range(DOCS):
        note = jnp.where(sub == i, slot_of(corpus_ref[i] // DOCS), note)
        note = jnp.where(sub == DOCS + i, corpus_ref[i] % DOCS + 1, note)
    docs_ref[:, pairs // 2 * LANES :] = note.astype(F32).astype(BF16)


def features_and_docs(own, other, lengths, corpus):
    smem = pl.BlockSpec(memory_space=pltpu.SMEM)
    vmem = pl.BlockSpec(memory_space=VMEM)
    return pl.pallas_call(
        docs_kernel,
        in_specs=[vmem, vmem, smem, smem],
        out_specs=[vmem, vmem],
        out_shape=[
            jax.ShapeDtypeStruct((TOK, 2 * RANK), BF16),
            jax.ShapeDtypeStruct((2 * DOCS, 9 * LANES), BF16),
        ],
        scratch_shapes=[VMEM((LANES + 16, LANES), F32)],
        compiler_params=params(),
        cost_estimate=pl.CostEstimate(flops=200_000_000, bytes_accessed=1_500_000, transcendentals=0),
    )(own, other, lengths, corpus)


def score_kernel(d0, d1, d2, d3, queries_ref, out_ref):
    width = 8 * LANES
    rows = queries_ref[...].reshape(LANES, 2 * width)
    left, right = rows[:, :width], rows[:, width:]
    for i, ref in enumerate((d0, d1, d2, d3)):
        piece = ref[:, :width]
        out_ref[i * DOCS : (i + 1) * DOCS, :] = (
            dot(piece, left, NT)[:DOCS] + dot(piece, right, NT)[DOCS:]
        )


def partial_scores(pieces, queries):
    vmem = pl.BlockSpec(memory_space=VMEM)
    return pl.pallas_call(
        score_kernel,
        in_specs=[vmem] * 5,
        out_specs=vmem,
        out_shape=jax.ShapeDtypeStruct((GROUP * DOCS, LANES), F32),
        compiler_params=params(),
        cost_estimate=pl.CostEstimate(flops=17_000_000, bytes_accessed=700_000, transcendentals=0),
    )(*pieces, queries)


def place_kernel(feat_ref, plan_ref, out_ref, tokens):
    me = lax.axis_index("mp")
    tokens[0:TOK, :] = feat_ref[...].astype(F32)
    lane = lane_iota((DP, LANES))
    dest = slot_of(plan_ref[:, 0:1])
    first = plan_ref[:, 1:2]
    send = jnp.where((dest == lane) & (first < CAP), 1.0, 0.0).astype(BF16)
    for r in range(HALF_BLOCK):
        rows = tokens[pl.ds(HALF_BLOCK * me + r, DP, stride=BLOCK), :].astype(BF16)
        out_ref[pl.ds(r, DP, stride=SLOT), :] = dot(send, rows, TN)
    for r in (SCORE_ROW, SCORE_ROW + 1, OWNER_ROW):
        out_ref[pl.ds(r, DP, stride=SLOT), :] = jnp.zeros((DP, LANES), F32)
    place = jnp.broadcast_to(first // BLOCK + 1, (DP, LANES)).astype(F32).astype(BF16)
    out_ref[pl.ds(PLACE_ROW, DP, stride=SLOT), :] = dot(send, place, TN)


def place_rows(features, plan):
    vmem = pl.BlockSpec(memory_space=VMEM)
    return pl.pallas_call(
        place_kernel,
        in_specs=[vmem] * 2,
        out_specs=vmem,
        out_shape=jax.ShapeDtypeStruct((DP * SLOT + PAD, LANES), F32),
        scratch_shapes=[VMEM((TOK + PAD, LANES), F32)],
        compiler_params=params(),
        cost_estimate=pl.CostEstimate(flops=20_000_000, bytes_accessed=900_000, transcendentals=0),
    )(features, plan)


def pack_kernel(base_ref, own_ref, other_ref, d0, d1, d2, d3, out_ref, stage):
    me = lax.axis_index("mp")
    stage[...] = base_ref[...]
    total = (own_ref[...] + other_ref[...]).astype(BF16).astype(F32)
    swapped = pltpu.roll(total, 64, 1)
    short = lane_iota(total.shape)
    piece = lax.broadcasted_iota(jnp.int32, total.shape, 0) // DOCS
    left = (short < 64) & (piece % 2 == 0)
    right = (short >= 64) & (piece % 2 == 1)
    scores = jnp.where(
        left,
        jnp.where(me == 0, total, swapped),
        jnp.where(right, jnp.where(me == 0, swapped, total), 0.0),
    ).astype(BF16)
    notes = [ref[:, 8 * LANES :].astype(F32) for ref in (d0, d1, d2, d3)]
    owner = jnp.concatenate([note[:DOCS] for note in notes], axis=0)
    row = jnp.concatenate([note[DOCS:] for note in notes], axis=0)
    hit = jnp.where(owner == short.astype(F32), 1.0, 0.0).astype(BF16)
    marks = jnp.where(short // 32 == piece, row, 0.0).astype(BF16)
    two = 2 * DOCS
    stage[pl.ds(SCORE_ROW, DP, stride=SLOT), :] = dot(hit[:two], scores[:two], TN)
    stage[pl.ds(SCORE_ROW + 1, DP, stride=SLOT), :] = dot(hit[two:], scores[two:], TN)
    stage[pl.ds(OWNER_ROW, DP, stride=SLOT), :] = dot(hit, marks, TN)
    out_ref[...] = stage[0 : DP * SLOT, :].astype(BF16)


def pack(base, own, other, pieces):
    vmem = pl.BlockSpec(memory_space=VMEM)
    return pl.pallas_call(
        pack_kernel,
        in_specs=[vmem] * 7,
        out_specs=vmem,
        out_shape=jax.ShapeDtypeStruct((DP * SLOT, LANES), BF16),
        scratch_shapes=[VMEM((DP * SLOT + PAD, LANES), F32)],
        compiler_params=params(),
        cost_estimate=pl.CostEstimate(flops=4_000_000, bytes_accessed=900_000, transcendentals=0),
    )(base, own, other, *pieces)


def split_kernel(got_ref, after_ref, rows_ref, notes_ref, stage):
    stage[0 : DP * SLOT, :] = got_ref[...].astype(F32)
    for r in range(HALF_BLOCK):
        part = stage[pl.ds(r, DP, stride=SLOT), :]
        rows_ref[r * DP : (r + 1) * DP, :] = part.astype(BF16)
    for r in range(HALF_BLOCK, SLOT):
        part = stage[pl.ds(r, DP, stride=SLOT), :]
        notes_ref[(r - HALF_BLOCK) * DP : (r - HALF_BLOCK + 1) * DP, :] = part


def split(got, after):
    vmem = pl.BlockSpec(memory_space=VMEM)
    return pl.pallas_call(
        split_kernel,
        in_specs=[vmem, pl.BlockSpec(memory_space=pl.ANY)],
        out_specs=[vmem, vmem],
        out_shape=[
            jax.ShapeDtypeStruct((HALF_BLOCK * DP, LANES), BF16),
            jax.ShapeDtypeStruct((HALF_BLOCK * DP, LANES), F32),
        ],
        scratch_shapes=[VMEM((DP * SLOT + PAD, LANES), F32)],
        compiler_params=params(),
        cost_estimate=pl.CostEstimate(flops=0, bytes_accessed=600_000, transcendentals=0),
    )(got, after)


def influence_kernel(notes_ref, influence_ref):
    count = DP // GROUP
    short = lane_iota((count, LANES))
    want = jnp.where(short % 32 < DOCS, short % 32 + 1, -1).astype(F32)
    low = lane_iota((DOCS, LANES)) < 64
    parts = []
    for x in range(GROUP):

        def taken(row):
            return notes_ref[pl.ds((row - HALF_BLOCK) * DP + x * count, count), :]

        hit = jnp.where(taken(OWNER_ROW) == want, 1.0, 0.0).astype(BF16)
        one = dot(hit, taken(SCORE_ROW).astype(BF16), TN)
        two = dot(hit, taken(SCORE_ROW + 1).astype(BF16), TN)
        parts.append(
            jnp.where(low, one[0:8] + two[64:72], one[32:40] + two[96:104]).astype(BF16)
        )
    source = lax.broadcasted_iota(jnp.int32, (GROUP * LANES, 2 * LANES), 0)
    column = lane_iota((GROUP * LANES, 2 * LANES))
    target = source % 64 // 4 * 16 + (GROUP - 1 - source // LANES) * 4 + source % 4
    order = jnp.where(column == target, 1.0, 0.0).astype(BF16)
    influence_ref[...] = dot(jnp.concatenate(parts, axis=1), order)


def influence_rows(notes):
    vmem = pl.BlockSpec(memory_space=VMEM)
    return pl.pallas_call(
        influence_kernel,
        in_specs=[vmem],
        out_specs=vmem,
        out_shape=jax.ShapeDtypeStruct((DOCS, 2 * LANES), F32),
        compiler_params=params(),
        cost_estimate=pl.CostEstimate(flops=2_000_000, bytes_accessed=270_000, transcendentals=0),
    )(notes)


def balance_kernel(own_ref, other_ref, notes_ref, balanced_ref, rows):
    me = lax.axis_index("mp")
    lane = lane_iota((DP, LANES))
    place = notes_ref[(PLACE_ROW - HALF_BLOCK) * DP : (PLACE_ROW - HALF_BLOCK + 1) * DP, :]
    put = jnp.where(place == (lane + 1).astype(F32), 1.0, 0.0).astype(BF16)
    blocks = CAP // BLOCK
    for r in range(HALF_BLOCK):
        near = own_ref[r * DP : (r + 1) * DP, :]
        far = other_ref[r * DP : (r + 1) * DP, :]
        rows[pl.ds(HALF_BLOCK * me + r, blocks, stride=BLOCK), :] = dot(put, near, TN)[:blocks]
        rows[pl.ds(HALF_BLOCK * (1 - me) + r, blocks, stride=BLOCK), :] = dot(put, far, TN)[:blocks]
    balanced_ref[...] = rows[0:CAP, :].astype(BF16)


def balance(own, other, notes):
    vmem = pl.BlockSpec(memory_space=VMEM)
    return pl.pallas_call(
        balance_kernel,
        in_specs=[vmem, vmem, vmem],
        out_specs=vmem,
        out_shape=jax.ShapeDtypeStruct((CAP, 2 * RANK), BF16),
        scratch_shapes=[VMEM((CAP + PAD, LANES), F32)],
        compiler_params=params(),
        cost_estimate=pl.CostEstimate(flops=40_000_000, bytes_accessed=700_000, transcendentals=0),
    )(own, other, notes)


def grad_kernel(own_ref, other_ref, weight_ref, out_ref, token_ref):
    half = own_ref.shape[1]
    me = lax.axis_index("mp")
    mine = weight_ref[pl.ds(pl.multiple_of(me * half, half), half), :]
    theirs = weight_ref[pl.ds(pl.multiple_of((1 - me) * half, half), half), :]
    total = dot(own_ref[...], mine) + dot(other_ref[...], theirs)
    out_ref[...] = total.astype(BF16)
    token_ref[...] = jnp.zeros_like(token_ref)


def input_gradient(own, other, weight):
    columns = 512
    return pl.pallas_call(
        grad_kernel,
        grid=(weight.shape[1] // columns,),
        in_specs=[
            pl.BlockSpec(own.shape, lambda j: (0, 0)),
            pl.BlockSpec(other.shape, lambda j: (0, 0)),
            pl.BlockSpec((weight.shape[0], columns), lambda j: (0, j)),
        ],
        out_specs=[
            pl.BlockSpec((TOK, columns), lambda j: (0, j)),
            pl.BlockSpec((8, LANES), lambda j: (0, 0)),
        ],
        out_shape=[
            jax.ShapeDtypeStruct((TOK, weight.shape[1]), BF16),
            jax.ShapeDtypeStruct((8, LANES), F32),
        ],
        compiler_params=params(),
        cost_estimate=pl.CostEstimate(flops=4_300_000_000, bytes_accessed=10_500_000, transcendentals=0),
    )(own, other, weight)


def body(
    acts, cotangent, value_weight, proj_in, proj_out, query_grads, lengths, plan, corpus, segments
):
    swap = [(0, 1), (1, 0)]
    members = DP // GROUP
    columns = [[k + GROUP * i for i in range(members)] for k in range(GROUP)]
    other_cot = lax.ppermute(cotangent, "mp", swap)
    queries = lax.all_to_all(
        copies(query_grads, members),
        "dp",
        0,
        0,
        tiled=True,
        axis_index_groups=columns,
    )
    own = partial_features(acts, cotangent, proj_in, proj_out)
    features, docs = features_and_docs(own, lax.ppermute(own, "mp", swap), lengths, corpus)
    pieces = [docs]
    for i in range(1, GROUP):
        pieces.append(lax.ppermute(docs, "dp", [(s, s ^ i) for s in range(DP)]))
    mine = partial_scores(pieces, queries)
    packed = pack(place_rows(features, plan), mine, lax.ppermute(mine, "mp", swap), pieces)
    got = lax.all_to_all(
        packed.reshape(DP, SLOT, LANES),
        "dp",
        0,
        0,
        tiled=True,
        axis_index_groups=[sorted(range(DP), key=slot_of)],
    )
    input_grad, token = input_gradient(cotangent, other_cot, value_weight)
    rows, notes = split(got.reshape(DP * SLOT, LANES), token)
    balanced = balance(rows, lax.ppermute(rows, "mp", swap), notes)
    influence = influence_rows(notes)
    return (input_grad, balanced, influence)


def solution(mesh):
    return jax.shard_map(
        body,
        mesh=mesh,
        in_specs=(
            P("dp", "mp"),
            P("dp", "mp"),
            P(None, "mp"),
            P(None, "mp"),
            P(),
            P("dp", "mp"),
            P("dp"),
            P("dp", None),
            P("dp"),
            P("dp"),
        ),
        out_specs=(P("dp", "mp"), P("dp", None), P("dp", "mp")),
        check_vma=False,
    )
```

```python
import jax
import jax.numpy as jnp
from jax import lax
from jax.experimental import pallas as pl
from jax.experimental.pallas import tpu as pltpu
from jax.sharding import PartitionSpec as P

BLOCK = 8
CAP = 640
DP = 128
TOK = 1024
RANK = 64
DOCS = 8
SLOT = 8
HALF_BLOCK = 4
SCORE_ROW = 4
PLACE_ROW = 6
OWNER_ROW = 7
GROUP = 4
PAD = 8
CHUNKS = ((0, 256), (256, 256), (512, 256), (768, 256))
LANES = 128
VMEM = pltpu.VMEM
F32 = jnp.float32
BF16 = jnp.bfloat16
NT = (((1,), (1,)), ((), ()))
TN = (((0,), (0,)), ((), ()))


def dot(a, b, dims=(((1,), (0,)), ((), ()))):
    return lax.dot_general(a, b, dims, preferred_element_type=F32)


def slot_of(device):
    z, y, x = device // 16, device // GROUP % GROUP, device % GROUP
    return DP - 1 - (x * 32 + (y + x) % 4 * 8 + (z + 2 * y + 3 * x) % 8)


def lane_iota(shape):
    return lax.broadcasted_iota(jnp.int32, shape, len(shape) - 1)


def params(mib=48):
    return pltpu.CompilerParams(vmem_limit_bytes=mib * 1024 * 1024)


def copies_kernel(source_ref, out_ref, held, sem, out_sem):
    load = pltpu.make_async_copy(source_ref, held, sem)
    load.start()
    load.wait()
    sends = [pltpu.make_async_copy(held, out_ref.at[i], out_sem) for i in range(out_ref.shape[0])]
    for send in sends:
        send.start()
    for send in sends:
        send.wait()


def copies(source, count):
    hbm = pl.BlockSpec(memory_space=pl.ANY)
    return pl.pallas_call(
        copies_kernel,
        in_specs=[hbm],
        out_specs=hbm,
        out_shape=pltpu.HBM((count,) + source.shape, source.dtype),
        scratch_shapes=[
            VMEM(source.shape, source.dtype),
            pltpu.SemaphoreType.DMA,
            pltpu.SemaphoreType.DMA,
        ],
        compiler_params=params(4),
    )(pltpu.with_memory_space_constraint(source, pltpu.HBM))


def partial_kernel(
    acts_ref, cot_ref, pin_ref, pout_ref, out_ref, acts, cot, pin, pout, in_sems
):
    half = cot_ref.shape[1]
    me = lax.axis_index("mp")
    weights = [
        pltpu.make_async_copy(pin_ref, pin, in_sems.at[0]),
        pltpu.make_async_copy(
            pout_ref.at[:, pl.ds(pl.multiple_of(me * half, half), half)], pout, in_sems.at[1]
        ),
    ]
    loads = []
    for i, (at, rows) in enumerate(CHUNKS):
        span = pl.ds(at, rows)
        loads.append(
            [
                pltpu.make_async_copy(acts_ref.at[span], acts.at[span], in_sems.at[2 + 2 * i]),
                pltpu.make_async_copy(cot_ref.at[span], cot.at[span], in_sems.at[3 + 2 * i]),
            ]
        )
    for copy in weights + loads[0] + loads[1]:
        copy.start()
    for copy in weights:
        copy.wait()
    for i, (at, rows) in enumerate(CHUNKS):
        span = pl.ds(at, rows)
        for copy in loads[i]:
            copy.wait()
        if i + 2 < len(CHUNKS):
            for copy in loads[i + 2]:
                copy.start()
        low = dot(acts[span, :], pin[...], NT)
        high = dot(cot[span, :], pout[...], NT)
        out_ref[span, :] = jnp.concatenate([low, high], axis=1).astype(BF16)


def partial_features(acts, cotangent, proj_in, proj_out):
    hbm = pl.BlockSpec(memory_space=pl.ANY)
    half = cotangent.shape[1]
    return pl.pallas_call(
        partial_kernel,
        in_specs=[hbm] * 4,
        out_specs=pl.BlockSpec(memory_space=VMEM),
        out_shape=VMEM((TOK, 2 * RANK), BF16),
        scratch_shapes=[
            VMEM(acts.shape, BF16),
            VMEM(cotangent.shape, BF16),
            VMEM(proj_in.shape, BF16),
            VMEM((RANK, half), BF16),
            pltpu.SemaphoreType.DMA((2 + 2 * len(CHUNKS),)),
        ],
        compiler_params=params(16),
        cost_estimate=pl.CostEstimate(flops=340_000_000, bytes_accessed=6_000_000, transcendentals=0),
    )(*(pltpu.with_memory_space_constraint(x, pltpu.HBM) for x in (acts, cotangent, proj_in, proj_out)))


def docs_kernel(own_ref, other_ref, lengths_ref, corpus_ref, feat_ref, docs_ref, scr):
    half = RANK // 2
    me = lax.axis_index("mp")
    feat = (own_ref[...].astype(F32) + other_ref[...].astype(F32)).astype(BF16)
    feat_ref[...] = feat
    wide = 2 * LANES
    row = lax.broadcasted_iota(jnp.int32, (wide, LANES), 0)
    want = RANK + me * half + 2 * (row % 16) + row // LANES
    pick = jnp.where(lane_iota((wide, LANES)) == want, 1.0, 0.0).astype(BF16)
    spread = dot(pick, feat, NT)
    doc = lax.broadcasted_iota(jnp.int32, (wide, 1), 0) % LANES // 16
    first = jnp.zeros((wide, 1), jnp.int32)
    last = jnp.zeros((wide, 1), jnp.int32)
    at = 0
    for i in range(DOCS):
        length = lengths_ref[i]
        first = jnp.where(doc == i, at, first)
        last = jnp.where(doc == i, at + length, last)
        at = at + length
    token = lane_iota((wide, TOK))
    live = (token >= first) & (token < last)
    both = dot(jnp.where(live, spread, 0.0).astype(BF16), feat)
    left = lane_iota((LANES, LANES)) < RANK
    scr[0:LANES, :] = jnp.where(left, both[:LANES], pltpu.roll(both[LANES:], RANK, 1))
    pairs = half // 2
    for p in range(pairs // 2):
        low = scr[pl.ds(p, DOCS, stride=pairs), :]
        high = scr[pl.ds(p + pairs // 2, DOCS, stride=pairs), :]
        docs_ref[:, p * LANES : (p + 1) * LANES] = jnp.concatenate([low, high], axis=0).astype(BF16)
    sub = lax.broadcasted_iota(jnp.int32, (2 * DOCS, LANES), 0)
    note = jnp.zeros((2 * DOCS, LANES), jnp.int32)
    for i in range(DOCS):
        note = jnp.where(sub == i, slot_of(corpus_ref[i] // DOCS), note)
        note = jnp.where(sub == DOCS + i, corpus_ref[i] % DOCS + 1, note)
    docs_ref[:, pairs // 2 * LANES :] = note.astype(F32).astype(BF16)


def features_and_docs(own, other, lengths, corpus):
    smem = pl.BlockSpec(memory_space=pltpu.SMEM)
    vmem = pl.BlockSpec(memory_space=VMEM)
    return pl.pallas_call(
        docs_kernel,
        in_specs=[vmem, vmem, smem, smem],
        out_specs=[vmem, vmem],
        out_shape=[
            jax.ShapeDtypeStruct((TOK, 2 * RANK), BF16),
            jax.ShapeDtypeStruct((2 * DOCS, 9 * LANES), BF16),
        ],
        scratch_shapes=[VMEM((LANES + 16, LANES), F32)],
        compiler_params=params(),
        cost_estimate=pl.CostEstimate(flops=200_000_000, bytes_accessed=1_500_000, transcendentals=0),
    )(own, other, lengths, corpus)


def score_kernel(d0, d1, d2, d3, queries_ref, out_ref):
    width = 8 * LANES
    rows = queries_ref[...].reshape(LANES, 2 * width)
    left, right = rows[:, :width], rows[:, width:]
    for i, ref in enumerate((d0, d1, d2, d3)):
        piece = ref[:, :width]
        out_ref[i * DOCS : (i + 1) * DOCS, :] = (
            dot(piece, left, NT)[:DOCS] + dot(piece, right, NT)[DOCS:]
        )


def partial_scores(pieces, queries):
    vmem = pl.BlockSpec(memory_space=VMEM)
    return pl.pallas_call(
        score_kernel,
        in_specs=[vmem] * 5,
        out_specs=vmem,
        out_shape=jax.ShapeDtypeStruct((GROUP * DOCS, LANES), F32),
        compiler_params=params(),
        cost_estimate=pl.CostEstimate(flops=17_000_000, bytes_accessed=700_000, transcendentals=0),
    )(*pieces, queries)


def place_kernel(feat_ref, plan_ref, out_ref, tokens):
    me = lax.axis_index("mp")
    tokens[0:TOK, :] = feat_ref[...].astype(F32)
    lane = lane_iota((DP, LANES))
    dest = slot_of(plan_ref[:, 0:1])
    first = plan_ref[:, 1:2]
    send = jnp.where((dest == lane) & (first < CAP), 1.0, 0.0).astype(BF16)
    for r in range(HALF_BLOCK):
        rows = tokens[pl.ds(HALF_BLOCK * me + r, DP, stride=BLOCK), :].astype(BF16)
        out_ref[pl.ds(r, DP, stride=SLOT), :] = dot(send, rows, TN)
    for r in (SCORE_ROW, SCORE_ROW + 1, OWNER_ROW):
        out_ref[pl.ds(r, DP, stride=SLOT), :] = jnp.zeros((DP, LANES), F32)
    place = jnp.broadcast_to(first // BLOCK + 1, (DP, LANES)).astype(F32).astype(BF16)
    out_ref[pl.ds(PLACE_ROW, DP, stride=SLOT), :] = dot(send, place, TN)


def place_rows(features, plan):
    vmem = pl.BlockSpec(memory_space=VMEM)
    return pl.pallas_call(
        place_kernel,
        in_specs=[vmem] * 2,
        out_specs=vmem,
        out_shape=jax.ShapeDtypeStruct((DP * SLOT + PAD, LANES), F32),
        scratch_shapes=[VMEM((TOK + PAD, LANES), F32)],
        compiler_params=params(),
        cost_estimate=pl.CostEstimate(flops=20_000_000, bytes_accessed=900_000, transcendentals=0),
    )(features, plan)


def pack_kernel(base_ref, own_ref, other_ref, d0, d1, d2, d3, out_ref, stage):
    me = lax.axis_index("mp")
    stage[...] = base_ref[...]
    sums = (own_ref[...] + other_ref[...]).astype(BF16)
    source = lax.broadcasted_iota(jnp.int32, (LANES, LANES), 0)
    z, y = 7 - source // 4 % 8, GROUP - 1 - source // 32
    order = lane_iota(source.shape) == (z * GROUP + y) * 4 + source % 4
    total = dot(sums, jnp.where(order, 1.0, 0.0).astype(BF16))
    swapped = pltpu.roll(total, 64, 1)
    short = lane_iota(total.shape)
    piece = lax.broadcasted_iota(jnp.int32, total.shape, 0) // DOCS
    left = (short < 64) & (piece % 2 == 0)
    right = (short >= 64) & (piece % 2 == 1)
    scores = jnp.where(
        left,
        jnp.where(me == 0, total, swapped),
        jnp.where(right, jnp.where(me == 0, swapped, total), 0.0),
    ).astype(BF16)
    notes = [ref[:, 8 * LANES :].astype(F32) for ref in (d0, d1, d2, d3)]
    owner = jnp.concatenate([note[:DOCS] for note in notes], axis=0)
    row = jnp.concatenate([note[DOCS:] for note in notes], axis=0)
    hit = jnp.where(owner == short.astype(F32), 1.0, 0.0).astype(BF16)
    marks = jnp.where(short // 32 == piece, row, 0.0).astype(BF16)
    two = 2 * DOCS
    stage[pl.ds(SCORE_ROW, DP, stride=SLOT), :] = dot(hit[:two], scores[:two], TN)
    stage[pl.ds(SCORE_ROW + 1, DP, stride=SLOT), :] = dot(hit[two:], scores[two:], TN)
    stage[pl.ds(OWNER_ROW, DP, stride=SLOT), :] = dot(hit, marks, TN)
    out_ref[...] = stage[0 : DP * SLOT, :].astype(BF16)


def pack(base, own, other, pieces):
    vmem = pl.BlockSpec(memory_space=VMEM)
    return pl.pallas_call(
        pack_kernel,
        in_specs=[vmem] * 7,
        out_specs=vmem,
        out_shape=jax.ShapeDtypeStruct((DP * SLOT, LANES), BF16),
        scratch_shapes=[VMEM((DP * SLOT + PAD, LANES), F32)],
        compiler_params=params(),
        cost_estimate=pl.CostEstimate(flops=4_000_000, bytes_accessed=900_000, transcendentals=0),
    )(base, own, other, *pieces)


def split_kernel(got_ref, after_ref, rows_ref, notes_ref, stage):
    stage[0 : DP * SLOT, :] = got_ref[...].astype(F32)
    for r in range(HALF_BLOCK):
        part = stage[pl.ds(r, DP, stride=SLOT), :]
        rows_ref[r * DP : (r + 1) * DP, :] = part.astype(BF16)
    for r in range(HALF_BLOCK, SLOT):
        part = stage[pl.ds(r, DP, stride=SLOT), :]
        notes_ref[(r - HALF_BLOCK) * DP : (r - HALF_BLOCK + 1) * DP, :] = part


def split(got, after):
    vmem = pl.BlockSpec(memory_space=VMEM)
    return pl.pallas_call(
        split_kernel,
        in_specs=[vmem, pl.BlockSpec(memory_space=pl.ANY)],
        out_specs=[vmem, vmem],
        out_shape=[
            jax.ShapeDtypeStruct((HALF_BLOCK * DP, LANES), BF16),
            jax.ShapeDtypeStruct((HALF_BLOCK * DP, LANES), F32),
        ],
        scratch_shapes=[VMEM((DP * SLOT + PAD, LANES), F32)],
        compiler_params=params(),
        cost_estimate=pl.CostEstimate(flops=0, bytes_accessed=600_000, transcendentals=0),
    )(got, after)


def influence_kernel(notes_ref, influence_ref):
    count = DP // GROUP
    short = lane_iota((count, LANES))
    want = jnp.where(short % 32 < DOCS, short % 32 + 1, -1).astype(F32)
    low = lane_iota((DOCS, LANES)) < 64
    parts = []
    for x in range(GROUP):

        def taken(row):
            return notes_ref[pl.ds((row - HALF_BLOCK) * DP + x * count, count), :]

        hit = jnp.where(taken(OWNER_ROW) == want, 1.0, 0.0).astype(BF16)
        one = dot(hit, taken(SCORE_ROW).astype(BF16), TN)
        two = dot(hit, taken(SCORE_ROW + 1).astype(BF16), TN)
        parts.append(
            jnp.where(low, one[0:8] + two[64:72], one[32:40] + two[96:104]).astype(BF16)
        )
    source = lax.broadcasted_iota(jnp.int32, (GROUP * LANES, 2 * LANES), 0)
    column = lane_iota((GROUP * LANES, 2 * LANES))
    target = source % 64 // 4 * 16 + (GROUP - 1 - source // LANES) * 4 + source % 4
    order = jnp.where(column == target, 1.0, 0.0).astype(BF16)
    influence_ref[...] = dot(jnp.concatenate(parts, axis=1), order)


def influence_rows(notes):
    vmem = pl.BlockSpec(memory_space=VMEM)
    return pl.pallas_call(
        influence_kernel,
        in_specs=[vmem],
        out_specs=vmem,
        out_shape=jax.ShapeDtypeStruct((DOCS, 2 * LANES), F32),
        compiler_params=params(),
        cost_estimate=pl.CostEstimate(flops=2_000_000, bytes_accessed=270_000, transcendentals=0),
    )(notes)


def balance_kernel(own_ref, other_ref, notes_ref, balanced_ref, rows):
    me = lax.axis_index("mp")
    lane = lane_iota((DP, LANES))
    place = notes_ref[(PLACE_ROW - HALF_BLOCK) * DP : (PLACE_ROW - HALF_BLOCK + 1) * DP, :]
    put = jnp.where(place == (lane + 1).astype(F32), 1.0, 0.0).astype(BF16)
    blocks = CAP // BLOCK
    for r in range(HALF_BLOCK):
        near = own_ref[r * DP : (r + 1) * DP, :]
        far = other_ref[r * DP : (r + 1) * DP, :]
        rows[pl.ds(HALF_BLOCK * me + r, blocks, stride=BLOCK), :] = dot(put, near, TN)[:blocks]
        rows[pl.ds(HALF_BLOCK * (1 - me) + r, blocks, stride=BLOCK), :] = dot(put, far, TN)[:blocks]
    balanced_ref[...] = rows[0:CAP, :].astype(BF16)


def balance(own, other, notes):
    vmem = pl.BlockSpec(memory_space=VMEM)
    return pl.pallas_call(
        balance_kernel,
        in_specs=[vmem, vmem, vmem],
        out_specs=vmem,
        out_shape=jax.ShapeDtypeStruct((CAP, 2 * RANK), BF16),
        scratch_shapes=[VMEM((CAP + PAD, LANES), F32)],
        compiler_params=params(),
        cost_estimate=pl.CostEstimate(flops=40_000_000, bytes_accessed=700_000, transcendentals=0),
    )(own, other, notes)


def grad_kernel(own_ref, other_ref, weight_ref, out_ref, token_ref):
    half = own_ref.shape[1]
    me = lax.axis_index("mp")
    mine = weight_ref[pl.ds(pl.multiple_of(me * half, half), half), :]
    theirs = weight_ref[pl.ds(pl.multiple_of((1 - me) * half, half), half), :]
    total = dot(own_ref[...], mine) + dot(other_ref[...], theirs)
    out_ref[...] = total.astype(BF16)
    token_ref[...] = jnp.zeros_like(token_ref)


def input_gradient(own, other, weight):
    columns = 512
    return pl.pallas_call(
        grad_kernel,
        grid=(weight.shape[1] // columns,),
        in_specs=[
            pl.BlockSpec(own.shape, lambda j: (0, 0)),
            pl.BlockSpec(other.shape, lambda j: (0, 0)),
            pl.BlockSpec((weight.shape[0], columns), lambda j: (0, j)),
        ],
        out_specs=[
            pl.BlockSpec((TOK, columns), lambda j: (0, j)),
            pl.BlockSpec((8, LANES), lambda j: (0, 0)),
        ],
        out_shape=[
            jax.ShapeDtypeStruct((TOK, weight.shape[1]), BF16),
            jax.ShapeDtypeStruct((8, LANES), F32),
        ],
        compiler_params=params(),
        cost_estimate=pl.CostEstimate(flops=4_300_000_000, bytes_accessed=10_500_000, transcendentals=0),
    )(own, other, weight)


def body(
    acts, cotangent, value_weight, proj_in, proj_out, query_grads, lengths, plan, corpus, segments
):
    swap = [(0, 1), (1, 0)]
    members = DP // GROUP
    columns = [
        [k + GROUP * y + GROUP * GROUP * z for y in reversed(range(GROUP)) for z in reversed(range(8))]
        for k in range(GROUP)
    ]
    other_cot = lax.ppermute(cotangent, "mp", swap)
    queries = lax.all_to_all(
        copies(query_grads, members),
        "dp",
        0,
        0,
        tiled=True,
        axis_index_groups=columns,
    )
    own = partial_features(acts, cotangent, proj_in, proj_out)
    features, docs = features_and_docs(own, lax.ppermute(own, "mp", swap), lengths, corpus)
    pieces = [docs]
    for i in range(1, GROUP):
        pieces.append(lax.ppermute(docs, "dp", [(s, s ^ i) for s in range(DP)]))
    mine = partial_scores(pieces, queries)
    packed = pack(place_rows(features, plan), mine, lax.ppermute(mine, "mp", swap), pieces)
    got = lax.all_to_all(
        packed.reshape(DP, SLOT, LANES),
        "dp",
        0,
        0,
        tiled=True,
        axis_index_groups=[sorted(range(DP), key=slot_of)],
    )
    input_grad, token = input_gradient(cotangent, other_cot, value_weight)
    rows, notes = split(got.reshape(DP * SLOT, LANES), token)
    balanced = balance(rows, lax.ppermute(rows, "mp", swap), notes)
    influence = influence_rows(notes)
    return (input_grad, balanced, influence)


def solution(mesh):
    return jax.shard_map(
        body,
        mesh=mesh,
        in_specs=(
            P("dp", "mp"),
            P("dp", "mp"),
            P(None, "mp"),
            P(None, "mp"),
            P(),
            P("dp", "mp"),
            P("dp"),
            P("dp", None),
            P("dp"),
            P("dp"),
        ),
        out_specs=(P("dp", "mp"), P("dp", None), P("dp", "mp")),
        check_vma=False,
    )
```

```python
import jax
import jax.numpy as jnp
from jax import lax
from jax.experimental import pallas as pl
from jax.experimental.pallas import tpu as pltpu
from jax.sharding import PartitionSpec as P

BLOCK = 8
CAP = 640
DP = 128
TOK = 1024
RANK = 64
DOCS = 8
SLOT = 8
HALF_BLOCK = 4
SCORE_ROW = 4
PLACE_ROW = 6
OWNER_ROW = 7
GROUP = 4
PAD = 8
CHUNKS = ((0, 256), (256, 256), (512, 256), (768, 256))
LANES = 128
VMEM = pltpu.VMEM
F32 = jnp.float32
BF16 = jnp.bfloat16
NT = (((1,), (1,)), ((), ()))
TN = (((0,), (0,)), ((), ()))


def dot(a, b, dims=(((1,), (0,)), ((), ()))):
    return lax.dot_general(a, b, dims, preferred_element_type=F32)


def slot_of(device):
    z, y, x = device // 16, device // GROUP % GROUP, device % GROUP
    return DP - 1 - (x * 32 + (y + x) % 4 * 8 + (z + 2 * y + 3 * x) % 8)


def lane_iota(shape):
    return lax.broadcasted_iota(jnp.int32, shape, len(shape) - 1)


def params(mib=48):
    return pltpu.CompilerParams(vmem_limit_bytes=mib * 1024 * 1024)


def copies_kernel(source_ref, out_ref, held, sem, out_sem):
    load = pltpu.make_async_copy(source_ref, held, sem)
    load.start()
    load.wait()
    sends = [pltpu.make_async_copy(held, out_ref.at[i], out_sem) for i in range(out_ref.shape[0])]
    for send in sends:
        send.start()
    for send in sends:
        send.wait()


def copies(source, count):
    hbm = pl.BlockSpec(memory_space=pl.ANY)
    return pl.pallas_call(
        copies_kernel,
        in_specs=[hbm],
        out_specs=hbm,
        out_shape=pltpu.HBM((count,) + source.shape, source.dtype),
        scratch_shapes=[
            VMEM(source.shape, source.dtype),
            pltpu.SemaphoreType.DMA,
            pltpu.SemaphoreType.DMA,
        ],
        compiler_params=params(4),
    )(pltpu.with_memory_space_constraint(source, pltpu.HBM))


def partial_kernel(
    acts_ref, cot_ref, pin_ref, pout_ref, out_ref, acts, cot, pin, pout, in_sems
):
    half = cot_ref.shape[1]
    me = lax.axis_index("mp")
    weights = [
        pltpu.make_async_copy(pin_ref, pin, in_sems.at[0]),
        pltpu.make_async_copy(
            pout_ref.at[:, pl.ds(pl.multiple_of(me * half, half), half)], pout, in_sems.at[1]
        ),
    ]
    loads = []
    for i, (at, rows) in enumerate(CHUNKS):
        span = pl.ds(at, rows)
        loads.append(
            [
                pltpu.make_async_copy(acts_ref.at[span], acts.at[span], in_sems.at[2 + 2 * i]),
                pltpu.make_async_copy(cot_ref.at[span], cot.at[span], in_sems.at[3 + 2 * i]),
            ]
        )
    for copy in weights + loads[0] + loads[1]:
        copy.start()
    for copy in weights:
        copy.wait()
    for i, (at, rows) in enumerate(CHUNKS):
        span = pl.ds(at, rows)
        for copy in loads[i]:
            copy.wait()
        if i + 2 < len(CHUNKS):
            for copy in loads[i + 2]:
                copy.start()
        low = dot(acts[span, :], pin[...], NT)
        high = dot(cot[span, :], pout[...], NT)
        out_ref[span, :] = jnp.concatenate([low, high], axis=1)


def partial_features(acts, cotangent, proj_in, proj_out):
    hbm = pl.BlockSpec(memory_space=pl.ANY)
    half = cotangent.shape[1]
    return pl.pallas_call(
        partial_kernel,
        in_specs=[hbm] * 4,
        out_specs=pl.BlockSpec(memory_space=VMEM),
        out_shape=VMEM((TOK, 2 * RANK), F32),
        scratch_shapes=[
            VMEM(acts.shape, BF16),
            VMEM(cotangent.shape, BF16),
            VMEM(proj_in.shape, BF16),
            VMEM((RANK, half), BF16),
            pltpu.SemaphoreType.DMA((2 + 2 * len(CHUNKS),)),
        ],
        compiler_params=params(16),
        cost_estimate=pl.CostEstimate(flops=340_000_000, bytes_accessed=6_000_000, transcendentals=0),
    )(*(pltpu.with_memory_space_constraint(x, pltpu.HBM) for x in (acts, cotangent, proj_in, proj_out)))


def docs_kernel(own_ref, other_ref, lengths_ref, corpus_ref, feat_ref, docs_ref, scr):
    half = RANK // 2
    me = lax.axis_index("mp")
    feat = (own_ref[...].astype(F32) + other_ref[...].astype(F32)).astype(BF16)
    feat_ref[...] = feat
    wide = 2 * LANES
    row = lax.broadcasted_iota(jnp.int32, (wide, LANES), 0)
    want = RANK + me * half + 2 * (row % 16) + row // LANES
    pick = jnp.where(lane_iota((wide, LANES)) == want, 1.0, 0.0).astype(BF16)
    spread = dot(pick, feat, NT)
    doc = lax.broadcasted_iota(jnp.int32, (wide, 1), 0) % LANES // 16
    first = jnp.zeros((wide, 1), jnp.int32)
    last = jnp.zeros((wide, 1), jnp.int32)
    at = 0
    for i in range(DOCS):
        length = lengths_ref[i]
        first = jnp.where(doc == i, at, first)
        last = jnp.where(doc == i, at + length, last)
        at = at + length
    token = lane_iota((wide, TOK))
    live = (token >= first) & (token < last)
    both = dot(jnp.where(live, spread, 0.0).astype(BF16), feat)
    left = lane_iota((LANES, LANES)) < RANK
    scr[0:LANES, :] = jnp.where(left, both[:LANES], pltpu.roll(both[LANES:], RANK, 1))
    pairs = half // 2
    for p in range(pairs // 2):
        low = scr[pl.ds(p, DOCS, stride=pairs), :]
        high = scr[pl.ds(p + pairs // 2, DOCS, stride=pairs), :]
        docs_ref[:, p * LANES : (p + 1) * LANES] = jnp.concatenate([low, high], axis=0).astype(BF16)
    sub = lax.broadcasted_iota(jnp.int32, (2 * DOCS, LANES), 0)
    note = jnp.zeros((2 * DOCS, LANES), jnp.int32)
    for i in range(DOCS):
        note = jnp.where(sub == i, slot_of(corpus_ref[i] // DOCS), note)
        note = jnp.where(sub == DOCS + i, corpus_ref[i] % DOCS + 1, note)
    docs_ref[:, pairs // 2 * LANES :] = note.astype(F32).astype(BF16)


def features_and_docs(own, other, lengths, corpus):
    smem = pl.BlockSpec(memory_space=pltpu.SMEM)
    vmem = pl.BlockSpec(memory_space=VMEM)
    return pl.pallas_call(
        docs_kernel,
        in_specs=[vmem, vmem, smem, smem],
        out_specs=[vmem, vmem],
        out_shape=[
            jax.ShapeDtypeStruct((TOK, 2 * RANK), BF16),
            jax.ShapeDtypeStruct((2 * DOCS, 9 * LANES), BF16),
        ],
        scratch_shapes=[VMEM((LANES + 16, LANES), F32)],
        compiler_params=params(),
        cost_estimate=pl.CostEstimate(flops=200_000_000, bytes_accessed=1_500_000, transcendentals=0),
    )(own, other, lengths, corpus)


def score_kernel(d0, d1, d2, d3, queries_ref, out_ref):
    width = 8 * LANES
    rows = queries_ref[...].reshape(LANES, 2 * width)
    left, right = rows[:, :width], rows[:, width:]
    for i, ref in enumerate((d0, d1, d2, d3)):
        piece = ref[:, :width]
        out_ref[i * DOCS : (i + 1) * DOCS, :] = (
            dot(piece, left, NT)[:DOCS] + dot(piece, right, NT)[DOCS:]
        )


def partial_scores(pieces, queries):
    vmem = pl.BlockSpec(memory_space=VMEM)
    return pl.pallas_call(
        score_kernel,
        in_specs=[vmem] * 5,
        out_specs=vmem,
        out_shape=jax.ShapeDtypeStruct((GROUP * DOCS, LANES), F32),
        compiler_params=params(),
        cost_estimate=pl.CostEstimate(flops=17_000_000, bytes_accessed=700_000, transcendentals=0),
    )(*pieces, queries)


def place_kernel(feat_ref, plan_ref, out_ref, tokens):
    me = lax.axis_index("mp")
    tokens[0:TOK, :] = feat_ref[...].astype(F32)
    lane = lane_iota((DP, LANES))
    dest = slot_of(plan_ref[:, 0:1])
    first = plan_ref[:, 1:2]
    send = jnp.where((dest == lane) & (first < CAP), 1.0, 0.0).astype(BF16)
    for r in range(HALF_BLOCK):
        rows = tokens[pl.ds(HALF_BLOCK * me + r, DP, stride=BLOCK), :].astype(BF16)
        out_ref[pl.ds(r, DP, stride=SLOT), :] = dot(send, rows, TN)
    for r in (SCORE_ROW, SCORE_ROW + 1, OWNER_ROW):
        out_ref[pl.ds(r, DP, stride=SLOT), :] = jnp.zeros((DP, LANES), F32)
    place = jnp.broadcast_to(first // BLOCK + 1, (DP, LANES)).astype(F32).astype(BF16)
    out_ref[pl.ds(PLACE_ROW, DP, stride=SLOT), :] = dot(send, place, TN)


def place_rows(features, plan):
    vmem = pl.BlockSpec(memory_space=VMEM)
    return pl.pallas_call(
        place_kernel,
        in_specs=[vmem] * 2,
        out_specs=vmem,
        out_shape=jax.ShapeDtypeStruct((DP * SLOT + PAD, LANES), F32),
        scratch_shapes=[VMEM((TOK + PAD, LANES), F32)],
        compiler_params=params(),
        cost_estimate=pl.CostEstimate(flops=20_000_000, bytes_accessed=900_000, transcendentals=0),
    )(features, plan)


def pack_kernel(base_ref, own_ref, other_ref, d0, d1, d2, d3, out_ref, stage):
    me = lax.axis_index("mp")
    stage[...] = base_ref[...]
    sums = (own_ref[...] + other_ref[...]).astype(BF16)
    source = lax.broadcasted_iota(jnp.int32, (LANES, LANES), 0)
    z, y = 7 - source // 4 % 8, GROUP - 1 - source // 32
    order = lane_iota(source.shape) == (z * GROUP + y) * 4 + source % 4
    total = dot(sums, jnp.where(order, 1.0, 0.0).astype(BF16))
    swapped = pltpu.roll(total, 64, 1)
    short = lane_iota(total.shape)
    piece = lax.broadcasted_iota(jnp.int32, total.shape, 0) // DOCS
    left = (short < 64) & (piece % 2 == 0)
    right = (short >= 64) & (piece % 2 == 1)
    scores = jnp.where(
        left,
        jnp.where(me == 0, total, swapped),
        jnp.where(right, jnp.where(me == 0, swapped, total), 0.0),
    ).astype(BF16)
    notes = [ref[:, 8 * LANES :].astype(F32) for ref in (d0, d1, d2, d3)]
    owner = jnp.concatenate([note[:DOCS] for note in notes], axis=0)
    row = jnp.concatenate([note[DOCS:] for note in notes], axis=0)
    hit = jnp.where(owner == short.astype(F32), 1.0, 0.0).astype(BF16)
    marks = jnp.where(short // 32 == piece, row, 0.0).astype(BF16)
    two = 2 * DOCS
    stage[pl.ds(SCORE_ROW, DP, stride=SLOT), :] = dot(hit[:two], scores[:two], TN)
    stage[pl.ds(SCORE_ROW + 1, DP, stride=SLOT), :] = dot(hit[two:], scores[two:], TN)
    stage[pl.ds(OWNER_ROW, DP, stride=SLOT), :] = dot(hit, marks, TN)
    out_ref[...] = stage[0 : DP * SLOT, :].astype(BF16)


def pack(base, own, other, pieces):
    vmem = pl.BlockSpec(memory_space=VMEM)
    return pl.pallas_call(
        pack_kernel,
        in_specs=[vmem] * 7,
        out_specs=vmem,
        out_shape=jax.ShapeDtypeStruct((DP * SLOT, LANES), BF16),
        scratch_shapes=[VMEM((DP * SLOT + PAD, LANES), F32)],
        compiler_params=params(),
        cost_estimate=pl.CostEstimate(flops=4_000_000, bytes_accessed=900_000, transcendentals=0),
    )(base, own, other, *pieces)


def split_kernel(got_ref, after_ref, rows_ref, notes_ref, stage):
    stage[0 : DP * SLOT, :] = got_ref[...].astype(F32)
    for r in range(HALF_BLOCK):
        part = stage[pl.ds(r, DP, stride=SLOT), :]
        rows_ref[r * DP : (r + 1) * DP, :] = part.astype(BF16)
    for r in range(HALF_BLOCK, SLOT):
        part = stage[pl.ds(r, DP, stride=SLOT), :]
        notes_ref[(r - HALF_BLOCK) * DP : (r - HALF_BLOCK + 1) * DP, :] = part


def split(got, after):
    vmem = pl.BlockSpec(memory_space=VMEM)
    return pl.pallas_call(
        split_kernel,
        in_specs=[vmem, pl.BlockSpec(memory_space=pl.ANY)],
        out_specs=[vmem, vmem],
        out_shape=[
            jax.ShapeDtypeStruct((HALF_BLOCK * DP, LANES), BF16),
            jax.ShapeDtypeStruct((HALF_BLOCK * DP, LANES), F32),
        ],
        scratch_shapes=[VMEM((DP * SLOT + PAD, LANES), F32)],
        compiler_params=params(),
        cost_estimate=pl.CostEstimate(flops=0, bytes_accessed=600_000, transcendentals=0),
    )(got, after)


def influence_kernel(notes_ref, influence_ref):
    count = DP // GROUP
    short = lane_iota((count, LANES))
    want = jnp.where(short % 32 < DOCS, short % 32 + 1, -1).astype(F32)
    low = lane_iota((DOCS, LANES)) < 64
    parts = []
    for x in range(GROUP):

        def taken(row):
            return notes_ref[pl.ds((row - HALF_BLOCK) * DP + x * count, count), :]

        hit = jnp.where(taken(OWNER_ROW) == want, 1.0, 0.0).astype(BF16)
        one = dot(hit, taken(SCORE_ROW).astype(BF16), TN)
        two = dot(hit, taken(SCORE_ROW + 1).astype(BF16), TN)
        parts.append(
            jnp.where(low, one[0:8] + two[64:72], one[32:40] + two[96:104]).astype(BF16)
        )
    source = lax.broadcasted_iota(jnp.int32, (GROUP * LANES, 2 * LANES), 0)
    column = lane_iota((GROUP * LANES, 2 * LANES))
    target = source % 64 // 4 * 16 + (GROUP - 1 - source // LANES) * 4 + source % 4
    order = jnp.where(column == target, 1.0, 0.0).astype(BF16)
    influence_ref[...] = dot(jnp.concatenate(parts, axis=1), order)


def influence_rows(notes):
    vmem = pl.BlockSpec(memory_space=VMEM)
    return pl.pallas_call(
        influence_kernel,
        in_specs=[vmem],
        out_specs=vmem,
        out_shape=jax.ShapeDtypeStruct((DOCS, 2 * LANES), F32),
        compiler_params=params(),
        cost_estimate=pl.CostEstimate(flops=2_000_000, bytes_accessed=270_000, transcendentals=0),
    )(notes)


def balance_kernel(own_ref, other_ref, notes_ref, balanced_ref, rows):
    me = lax.axis_index("mp")
    lane = lane_iota((DP, LANES))
    place = notes_ref[(PLACE_ROW - HALF_BLOCK) * DP : (PLACE_ROW - HALF_BLOCK + 1) * DP, :]
    put = jnp.where(place == (lane + 1).astype(F32), 1.0, 0.0).astype(BF16)
    blocks = CAP // BLOCK
    for r in range(HALF_BLOCK):
        near = own_ref[r * DP : (r + 1) * DP, :]
        far = other_ref[r * DP : (r + 1) * DP, :]
        rows[pl.ds(HALF_BLOCK * me + r, blocks, stride=BLOCK), :] = dot(put, near, TN)[:blocks]
        rows[pl.ds(HALF_BLOCK * (1 - me) + r, blocks, stride=BLOCK), :] = dot(put, far, TN)[:blocks]
    balanced_ref[...] = rows[0:CAP, :].astype(BF16)


def balance(own, other, notes):
    vmem = pl.BlockSpec(memory_space=VMEM)
    return pl.pallas_call(
        balance_kernel,
        in_specs=[vmem, vmem, vmem],
        out_specs=vmem,
        out_shape=jax.ShapeDtypeStruct((CAP, 2 * RANK), BF16),
        scratch_shapes=[VMEM((CAP + PAD, LANES), F32)],
        compiler_params=params(),
        cost_estimate=pl.CostEstimate(flops=40_000_000, bytes_accessed=700_000, transcendentals=0),
    )(own, other, notes)


def grad_kernel(own_ref, other_ref, weight_ref, out_ref, token_ref):
    half = own_ref.shape[1]
    me = lax.axis_index("mp")
    mine = weight_ref[pl.ds(pl.multiple_of(me * half, half), half), :]
    theirs = weight_ref[pl.ds(pl.multiple_of((1 - me) * half, half), half), :]
    total = dot(own_ref[...], mine) + dot(other_ref[...], theirs)
    out_ref[...] = total.astype(BF16)
    token_ref[...] = jnp.zeros_like(token_ref)


def input_gradient(own, other, weight):
    columns = 512
    return pl.pallas_call(
        grad_kernel,
        grid=(weight.shape[1] // columns,),
        in_specs=[
            pl.BlockSpec(own.shape, lambda j: (0, 0)),
            pl.BlockSpec(other.shape, lambda j: (0, 0)),
            pl.BlockSpec((weight.shape[0], columns), lambda j: (0, j)),
        ],
        out_specs=[
            pl.BlockSpec((TOK, columns), lambda j: (0, j)),
            pl.BlockSpec((8, LANES), lambda j: (0, 0)),
        ],
        out_shape=[
            jax.ShapeDtypeStruct((TOK, weight.shape[1]), BF16),
            jax.ShapeDtypeStruct((8, LANES), F32),
        ],
        compiler_params=params(),
        cost_estimate=pl.CostEstimate(flops=4_300_000_000, bytes_accessed=10_500_000, transcendentals=0),
    )(own, other, weight)


def body(
    acts, cotangent, value_weight, proj_in, proj_out, query_grads, lengths, plan, corpus, segments
):
    swap = [(0, 1), (1, 0)]
    members = DP // GROUP
    columns = [
        [k + GROUP * y + GROUP * GROUP * z for y in reversed(range(GROUP)) for z in reversed(range(8))]
        for k in range(GROUP)
    ]
    other_cot = lax.ppermute(cotangent, "mp", swap)
    queries = lax.all_to_all(
        copies(query_grads, members),
        "dp",
        0,
        0,
        tiled=True,
        axis_index_groups=columns,
    )
    own = partial_features(acts, cotangent, proj_in, proj_out)
    features, docs = features_and_docs(own, lax.ppermute(own, "mp", swap), lengths, corpus)
    pieces = [docs]
    for i in range(1, GROUP):
        pieces.append(lax.ppermute(docs, "dp", [(s, s ^ i) for s in range(DP)]))
    mine = partial_scores(pieces, queries)
    packed = pack(place_rows(features, plan), mine, lax.ppermute(mine, "mp", swap), pieces)
    got = lax.all_to_all(
        packed.reshape(DP, SLOT, LANES),
        "dp",
        0,
        0,
        tiled=True,
        axis_index_groups=[sorted(range(DP), key=slot_of)],
    )
    input_grad, token = input_gradient(cotangent, other_cot, value_weight)
    rows, notes = split(got.reshape(DP * SLOT, LANES), token)
    balanced = balance(rows, lax.ppermute(rows, "mp", swap), notes)
    influence = influence_rows(notes)
    return (input_grad, balanced, influence)


def solution(mesh):
    return jax.shard_map(
        body,
        mesh=mesh,
        in_specs=(
            P("dp", "mp"),
            P("dp", "mp"),
            P(None, "mp"),
            P(None, "mp"),
            P(),
            P("dp", "mp"),
            P("dp"),
            P("dp", None),
            P("dp"),
            P("dp"),
        ),
        out_specs=(P("dp", "mp"), P("dp", None), P("dp", "mp")),
        check_vma=False,
    )
```
